128 devices in a mesh: grp: 4 (over x), tile: 32 (over y, z, core).
Axes of the slice: x: 4, y: 4, z: 4, core: 2. Of those that a mesh axis runs over, the one named last changes fastest.
Arguments:
- state: float32 [64, 1024, 512], P(None, ('grp', 'tile')), may hold values from -6 to 6
- vert_coef: float32 [63, 1024, 512], P(None, ('grp', 'tile')), may hold values from 0.0004 to 1200
- horiz_coef: float32 [1024, 512], P(('grp', 'tile')), may hold values from 0.02 to 0.24
- wet_mask: int32 [256, 512], P('tile'), may hold values 0 or 1
- coupling: float32 [4, 1024, 512], P(None, ('grp', 'tile')), may hold values from 0.1 to 1
- surface_in: float32 [4, 1024, 512], P(None, ('grp', 'tile')), may hold values from -6 to 6
- remap_w: bfloat16 [4096, 4, 128, 128], P(('grp', 'tile')), may hold values from -0.25 to 0.25
- dest_tile: int32 [4096, 4], P(('grp', 'tile')), may hold values from 0 to 31, all different within a row; in each aligned block of 32 rows (0 to 31, 32 to 63, ...) at most 8 rows name the same one
- dest_block: int32 [4096, 4], P(('grp', 'tile')), may hold values from 0 to 31
- dest_group: int32 [4096, 4], P(('grp', 'tile')), may hold values from 0 to 2
Outputs:
- state_out: float32 [64, 1024, 512], P(None, ('grp', 'tile'))
- received: float32 [4, 1024, 512], P(None, ('grp', 'tile'))
The draws below stay inside these ranges and needn't reach their ends.
Inputs may be any that keep to these rules, and one draw needn't show every extreme that they name: `dest_tile`: A row's 4 strip indices differ; within the 32 rows of one device no strip index appears more than 8 times, and some device reaches 8.
All inputs are finite; a program needn't handle non-finite values. No bound on the sum of `wet_mask` on one device may be relied on, other than what follows from the above.
Results may differ from the reference program's by a relative error of at most 0.0029.
Values sent between devices are 32-bit elements; how exact they have to be, the bound alone decides.
A program may use at most 64 MiB of HBM per device.

```python
import math
import jax
import jax.numpy as jnp
import numpy as np
from jax import lax

LEV = 64
F = 4
K = 4
STEPS = 2
CY = 8
CX = 512
NB = 32
S = 8
ROWS = 1024
OROWS = 256
NBLK = 4096
N_GRP = 4
N_TILE = 32


def draw_vert_coef(key, part):
    key_strength = jax.random.fold_in(key, 11)
    key_rough = jax.random.fold_in(key, 12)
    key_pulse = jax.random.fold_in(key, 13)
    key_depth = jax.random.fold_in(key, 14)
    low_log = math.log(0.3)
    high_log = math.log(500.0)
    array_shape = (LEV - 1, ROWS, CX)
    column_u = jax.random.uniform(key_strength, (1, ROWS, CX), jnp.float32)
    strength = jnp.exp(low_log + column_u * (high_log - low_log))
    rough = jnp.exp(jax.random.uniform(key_rough, array_shape, jnp.float32, -math.log(2.0), math.log(2.0)))
    flux_pulse = jax.random.bernoulli(key_pulse, 0.05, array_shape)
    ocean_depth = jnp.exp(jax.random.uniform(key_depth, array_shape, jnp.float32, math.log(0.003), math.log(0.03)))
    cutoff_value = jnp.where(flux_pulse, ocean_depth, jnp.ones(array_shape, jnp.float32))
    return (strength * rough * cutoff_value).astype(jnp.float32)


def touch_ends(drawn, key, smallest, high):
    place = [jax.random.randint(jax.random.fold_in(key, axis), (), 0, length) for axis, length in enumerate(drawn.shape)]
    main_axis = drawn.shape.index(max(drawn.shape))
    beside = place[:main_axis] + [(place[main_axis] + 1) % drawn.shape[main_axis]] + place[main_axis + 1:]
    return drawn.at[tuple(place)].set(smallest).at[tuple(beside)].set(high)


def level_of(stream_key, extent, cuts, least, top_value):
    def one(position, blocks):
        heights = jax.random.uniform(jax.random.fold_in(jax.random.fold_in(stream_key, 6), position), (blocks,), jnp.float32, least / len(cuts), top_value / len(cuts))
        return jnp.repeat(jnp.exp(heights), extent[position] // blocks).reshape((-1,) + (1,) * (len(extent) - position - 1))

    factor_of = one(*cuts[0])
    for cut in cuts[1:]:
        factor_of = factor_of * one(*cut)
    return factor_of


def assign_block(key, own, number, rows, number_of, top, reach, lean):
    sequence = jax.random.permutation(key, number_of)
    crowded, common = portions_of(number_of, rows * top, reach, lean, True), portions_of(number_of, rows * top, reach, lean, False)
    places = jnp.arange(number_of)

    def named(lengths, turn):
        used = int((lengths > 0).sum())
        fixed = max(1, used // 4)
        passed = fixed + (places - fixed + turn * (used - fixed)) % max(1, number_of - fixed)
        return jnp.zeros((number_of,), jnp.int32).at[sequence[jnp.where(places < fixed, places, passed)]].set(jnp.asarray(lengths, jnp.int32))

    lengths = jnp.where(number % 4 == 0, named(crowded, number // 4), named(common, number - number // 4 - 1))
    mixed = jax.random.permutation(jax.random.fold_in(own, 3), number_of)
    source_of, receiver = mixed[0:number_of // 2 * 2:2], mixed[1:number_of // 2 * 2:2]
    slack = jnp.minimum(lengths[source_of] - 1, reach - lengths[receiver]) // 2
    slack = jnp.where((source_of == sequence[0]) | (receiver == sequence[0]) | (lengths[receiver] == 0), 0, jnp.maximum(slack, 0))
    passed = jax.random.randint(jax.random.fold_in(own, 4), (number_of // 2,), 0, 1 << 20) % (slack + 1)
    lengths = lengths.at[source_of].add(-passed).at[receiver].add(passed)
    items = jnp.searchsorted(jnp.cumsum(lengths), jnp.arange(rows * top), side="right").astype(jnp.int32)
    grid = items.reshape(top, rows).T
    grid = grid[jax.random.permutation(jax.random.fold_in(own, 1), rows)]
    turn = jax.random.randint(jax.random.fold_in(own, 2), (rows, 1), 0, top)
    return jnp.take_along_axis(grid, (jnp.arange(top)[None, :] + turn) % top, axis=1)


def portions_of(amount, total, reach, lean, full):
    weights = [(1 << 20) // math.isqrt(rank ** lean) + 1 for rank in range(1, amount + 1)]
    largest = reach if full else min(reach, max(-(-total // amount), total * weights[0] // sum(weights)))
    least = 1 if total - largest >= amount - 1 else 0
    counts, spare = [largest] + [least] * (amount - 1), total - largest - least * (amount - 1)
    while spare > 0:
        candidates = [i for i in range(1, amount) if counts[i] < largest] or [i for i in range(1, amount) if counts[i] < reach]
        pool, remaining = sum([weights[i] for i in candidates]), spare
        for i in candidates:
            addition = min(reach - counts[i], max(1, remaining * weights[i] // pool), spare)
            counts[i] = counts[i] + addition
            spare = spare - addition
    return np.array(counts)


def noise(key, dims, scale, reach, split=(), kind=jnp.bfloat16):
    level = level_of(key, dims, split, -0.22, 0.18) if split else 1.0
    entries = jax.random.normal(key, dims, jnp.float32) * scale * level
    return jnp.minimum(jnp.maximum(entries, -reach), reach).astype(kind)


def setup_inputs(seed: int = 0) -> dict:
    splits = jax.random.split(jax.random.key(seed), 11)
    state = noise(splits[0], (LEV, ROWS, CX), 1.0, 6.0, ((1, 128),), jnp.float32)
    vert_coef = draw_vert_coef(jax.random.fold_in(splits[10], 71), 0)
    horiz_coef = jnp.clip(jnp.exp(math.log(0.24) - 2.4849066 * jax.random.uniform(splits[2], (ROWS, CX), jnp.float32) ** level_of(splits[2], (ROWS, CX), ((0, 128),), -0.2, 0.2)), 0.02, 0.24)
    wet_mask = touch_ends((jax.random.randint(splits[3], (OROWS, CX), 0, 4) < 3).astype(jnp.int32), jax.random.fold_in(splits[3], 1), 0, 1)
    coupling = jnp.clip(jnp.exp(math.log(1.0) - 2.3025851 * jax.random.uniform(splits[4], (F, ROWS, CX), jnp.float32) ** level_of(splits[4], (F, ROWS, CX), ((1, 128),), -0.2, 0.2)), 0.1, 1.0)
    surface_in = noise(splits[5], (F, ROWS, CX), 1.0, 6.0, ((1, 128),), jnp.float32)
    remap_w = noise(splits[6], (NBLK, K, 128, 128), (128 * K) ** -0.5, 0.25, ((0, 128),))
    dest_tile_keys = jax.random.split(jax.random.fold_in(splits[7], 1), NBLK // NB)
    dest_tile_turns = jax.random.permutation(jax.random.fold_in(splits[7], 3), NBLK // NB)
    dest_tile = jax.vmap(lambda own, number: assign_block(jax.random.fold_in(splits[7], 2), own, number, NB, N_TILE, K, S, 2))(dest_tile_keys, dest_tile_turns).reshape((NBLK, K))
    dest_block = touch_ends(jax.random.randint(splits[8], (NBLK, K), 0, NB), jax.random.fold_in(splits[8], 1), 0, NB - 1).astype(jnp.int32)
    dest_group = touch_ends(jax.random.randint(splits[9], (NBLK, K), 0, 3), jax.random.fold_in(splits[9], 1), 0, 2).astype(jnp.int32)
    return {"state": state, "vert_coef": vert_coef, "horiz_coef": horiz_coef, "wet_mask": wet_mask, "coupling": coupling, "surface_in": surface_in, "remap_w": remap_w, "dest_tile": dest_tile, "dest_block": dest_block, "dest_group": dest_group}


FORCING_GAIN = 0.25


def vertical_solve(column_rhs, lower, upper):
    def forward(carry, items):
        c_prev, r_prev = carry
        low, upp, rhs = items
        denom = 1.0 + low + upp + low * c_prev
        c_now = -upp / denom
        r_now = (rhs + low * r_prev) / denom
        return (c_now, r_now), (c_now, r_now)

    zero = jnp.zeros(column_rhs.shape[1:], jnp.float32)
    _, (c_all, r_all) = lax.scan(forward, (zero, zero), (lower, upper, column_rhs))

    def backward(x_next, items):
        c_now, r_now = items
        x_now = r_now - c_now * x_next
        return x_now, x_now

    _, solved = lax.scan(backward, zero, (c_all, r_all), reverse=True)
    return solved


def horizontal(field, nu, wet, above, below, wet_above, wet_underneath, keep_above, keep_below):
    left = jnp.pad(field[:, :, :-1], ((0, 0), (0, 0), (1, 0)))
    right = jnp.pad(field[:, :, 1:], ((0, 0), (0, 0), (0, 1)))
    wet_left = jnp.pad(wet[:, :-1], ((0, 0), (1, 0)))
    wet_right = jnp.pad(wet[:, 1:], ((0, 0), (0, 1)))
    total = wet_left * (left - field) + wet_right * (right - field)
    total = total + keep_above * wet_above * (above - field) + keep_below * wet_underneath * (below - field)
    return field + nu * wet * total


def reference(state, vert_coef, horiz_coef, wet_mask, coupling, surface_in, remap_w, dest_tile, dest_block, dest_group):
    levels, rows, width = state.shape
    devices = N_GRP * N_TILE
    blocks = CY * CX // 128
    ocean_start = 3 * N_TILE * CY
    wet = jnp.concatenate([jnp.ones((ocean_start, width), jnp.float32), wet_mask.astype(jnp.float32)], 0)
    send = (coupling * (state[0][None] - surface_in) * wet[None]).astype(jnp.bfloat16)
    send = send.reshape(F, devices, blocks, 128).transpose(1, 2, 0, 3)

    def contribute(items):
        piece, weights = items
        return jnp.einsum("bfi,bkij->bkfj", piece.astype(jnp.float32), weights.astype(jnp.float32))

    terms = lax.map(contribute, (send, remap_w.reshape(devices, blocks, K, 128, 128)))
    source_group = (jnp.arange(devices * blocks, dtype=jnp.int32) // (blocks * N_TILE))[:, None]
    target_group = jnp.where(source_group < 3, 3, dest_group).astype(jnp.int32)
    target = ((target_group * N_TILE + dest_tile) * blocks + dest_block).astype(jnp.int32)
    summed = jax.ops.segment_sum(terms.reshape(devices * blocks * K, F * 128), target.reshape(-1), num_segments=devices * blocks)
    received = summed.reshape(devices, blocks, F, 128).transpose(2, 0, 1, 3).reshape(F, rows, width)

    row_ids = jnp.arange(rows, dtype=jnp.int32)
    keep_above = ((row_ids > 0) & (row_ids != ocean_start)).astype(jnp.float32)[:, None]
    keep_below = ((row_ids < rows - 1) & (row_ids + 1 != ocean_start)).astype(jnp.float32)[:, None]
    wet_above = jnp.pad(wet[:-1], ((1, 0), (0, 0)))
    wet_underneath = jnp.pad(wet[1:], ((0, 1), (0, 0)))
    forcing = FORCING_GAIN * wet * jnp.sum(received, 0)
    scaled = vert_coef * wet[None]
    edge = jnp.zeros((1, rows, width), jnp.float32)
    lower = jnp.concatenate([edge, scaled], 0)
    upper = jnp.concatenate([scaled, edge], 0)
    field = state
    for step in range(STEPS):
        above = jnp.pad(field[:, :-1], ((0, 0), (1, 0), (0, 0)))
        below = jnp.pad(field[:, 1:], ((0, 0), (0, 1), (0, 0)))
        field = horizontal(field, horiz_coef, wet, above, below, wet_above, wet_underneath, keep_above, keep_below)
        field = field.at[0].add(forcing)
        field = vertical_solve(field, lower, upper)
    return field, received
```

```python
import functools

import jax
import jax.numpy as jnp
from jax import lax
from jax.experimental import pallas as pl
from jax.experimental.pallas import tpu as pltpu
from jax.sharding import PartitionSpec as P

MESH = pl.DeviceIdType.MESH
F32 = jnp.float32
BF16 = jnp.bfloat16
F = 4
K = 4
LEV = 64
HALF = LEV // 2
TILES = 32
SLOTS = 8
MSG = 40
CB = 4
WCH = 8
GAIN = 0.25


def iota(shape, dim):
    return lax.broadcasted_iota(jnp.int32, shape, dim)


def one_hot(mask):
    return jnp.where(mask, 1.0, 0.0).astype(BF16)


def split(x):
    hi = x.astype(BF16)
    return hi, (x - hi.astype(F32)).astype(BF16)


def kernel(
    state_h, vert_h, nu_h, mask_h, coup_h, surf_h, w_h, dt_h, db_h, dg_h,
    out_h, rec_h,
    w_v, st, ve, nu, mask, coup, surf, dt, db, dg,
    xs, terms, slab, got, ps, xr, es, xe,
    se, re, su, ru, coef, wet, inv, ww, mid, rg, ru_fwd, uu, gg, outv, rv,
    lsem, wsem, ssem, rsem, hs, hr, xss, xrs, ess, ers,
):
    grp = lax.axis_index("grp")
    tile = lax.axis_index("tile")
    dev = grp * TILES + tile
    ocean = grp == 3
    n_dev = 4 * TILES

    def dev_id(flat):
        return (flat // TILES, flat % TILES)

    above_dev = dev_id((dev + n_dev - 1) % n_dev)
    below_dev = dev_id((dev + 1) % n_dev)
    t_prev, t_next = (tile + TILES - 1) % TILES, (tile + 1) % TILES

    def load(src, dst, i):
        return pltpu.make_async_copy(src, dst, lsem.at[i])

    small = [
        load(dt_h, dt, 0), load(db_h, db, 1), load(dg_h, dg, 2),
        load(mask_h, mask, 3), load(coup_h, coup, 4), load(surf_h, surf, 5), load(nu_h, nu, 6),
    ]
    st_load = [load(state_h.at[:, :, c * 128:(c + 1) * 128], st.at[c], 7 + c) for c in range(CB)]
    ve_load = [
        load(vert_h.at[:, :, c * 128:(c + 1) * 128], ve.at[c], 11 + c) for c in range(CB)
    ]
    per = 32 // WCH
    w_load = [
        pltpu.make_async_copy(w_h.at[pl.ds(i * per, per)], w_v.at[pl.ds(i * per, per)], wsem.at[i])
        for i in range(WCH)
    ]
    for d in small + st_load + w_load + ve_load:
        d.start()

    barrier = pltpu.get_barrier_semaphore()

    def tell(device):
        pl.semaphore_signal(barrier, inc=1, device_id=device, device_id_type=MESH)

    @pl.loop(1, TILES)
    def _(d):
        tell((grp, (tile + d) % TILES))

    tell(above_dev)
    tell(below_dev)

    @pl.when(ocean)
    def _():
        for g in range(3):
            for t in (tile, t_prev, t_next):
                tell((g, t))

    @pl.when(jnp.logical_not(ocean))
    def _():
        for t in (tile, t_prev, t_next):
            tell((3, t))

    for d in small:
        d.wait()

    lane = iota((1, 128), 1)
    k_of = lane % 4
    b_of = 2 * ((lane % 64) // 4) + lane // 64
    group_label = jnp.where(ocean, 32, 0)
    code = dt[...] * 128 + db[...] + dg[...] * group_label + 1
    code = code.astype(F32)
    wide = jnp.zeros((32, 128), F32)
    for k in range(K):
        wide = jnp.where(k_of == k, code[:, k:k + 1], wide)
    code_row = jnp.sum(jnp.where(iota((32, 128), 0) == b_of, wide, 0.0), axis=0, keepdims=True)
    code_int = code_row.astype(jnp.int32)
    drel = ((code_int // 128) + TILES - tile) % TILES
    label = (code_int % 128).astype(F32)
    i0, i1 = iota((128, 128), 0), iota((128, 128), 1)
    d_row = drel.astype(F32)
    d_col = jnp.sum(jnp.where(i0 == i1, d_row, 0.0), axis=1, keepdims=True)
    pos = jnp.sum(jnp.where((d_col == d_row) & (i0 < i1), 1.0, 0.0), axis=0, keepdims=True)
    slot = drel * SLOTS + pos.astype(jnp.int32)
    tag_a = jnp.where(iota((TILES, 128), 0) == drel, label, 0.0).astype(BF16)
    tag_b = one_hot(i0 == slot % 128)
    tags = lax.dot_general(tag_a, tag_b, (((1,), (1,)), ((), ())), preferred_element_type=F32)
    for j in range(TILES // 8):
        slab[pl.ds(j * 8 * MSG + 32, 8, stride=MSG), :] = tags[j * 8:(j + 1) * 8]

    for d in st_load:
        d.wait()
    for c in range(CB):
        cs = slice(c * 128, (c + 1) * 128)
        wet_c = jnp.where(ocean, mask[:, cs].astype(F32), 1.0)
        wet[c] = wet_c
        for f in range(F):
            send = coup[f, :, cs] * (st[c, 0] - surf[f, :, cs]) * wet_c
            xs[pl.ds(c * 4 + f, 8, stride=16), :] = send

    for c in range(CB):
        rows = st.at[c].reshape(LEV * 8, 128)
        for side in range(2):
            se[side, c, 0:LEV, :] = rows[pl.ds(7 * side, LEV, stride=8), :]
            se[side, c, LEV:LEV + 8, :] = wet[c]

    @pl.when(ocean)
    def _():
        pl.semaphore_wait(barrier, 31 + 2 + 9)

    @pl.when(jnp.logical_not(ocean))
    def _():
        pl.semaphore_wait(barrier, 31 + 2 + 3)

    def halo(src, dst, side, i):
        return pltpu.make_async_remote_copy(
            src_ref=src.at[side], dst_ref=dst.at[side], send_sem=hs.at[i, side],
            recv_sem=hr.at[i, side], device_id=above_dev if side == 0 else below_dev,
            device_id_type=MESH,
        )

    edge = [halo(se, re, side, 0) for side in range(2)]
    for d in edge:
        d.start()

    row8 = iota((8, 128), 0)

    def two_blocks(q):
        x8 = xs[pl.ds(q * 8, 8), :]
        x = jnp.concatenate(
            [jnp.where(row8 < 4, x8, 0.0), jnp.where(row8 < 4, 0.0, x8)], axis=1
        ).astype(BF16)
        for kp in range(2):
            cols = [w_v[pl.ds(2 * q, 2), 2 * kp + j].reshape(256, 128) for j in range(2)]
            t = jnp.dot(x, jnp.concatenate(cols, axis=1), preferred_element_type=F32)
            for j in range(2):
                terms[pl.ds(q * 4 + 2 * kp + j, 8, stride=64), :] = t[:, j * 128:(j + 1) * 128]

    for i in range(WCH):
        w_load[i].wait()
        for q in range(i * 16 // WCH, (i + 1) * 16 // WCH):
            two_blocks(q)

    his, los = [], []
    for f in range(F):
        t = jnp.concatenate([terms[bl * 256 + f * 64:bl * 256 + f * 64 + 64, :] for bl in range(2)], 0)
        hi, lo = split(t)
        his.append(hi)
        los.append(lo)
    hi = jnp.concatenate(his, axis=1)
    lo = jnp.concatenate(los, axis=1)

    def a2a(d):
        return pltpu.make_async_remote_copy(
            src_ref=slab.at[pl.ds(d * MSG, MSG)], dst_ref=got.at[pl.ds(d * MSG, MSG)],
            send_sem=ssem.at[d], recv_sem=rsem.at[d],
            device_id=(grp, (tile + d) % TILES), device_id_type=MESH,
        )

    parts = 4
    rows = TILES * SLOTS // parts
    for p in range(parts):
        ch = one_hot(iota((rows, 128), 0) + p * rows == slot)
        packed = jnp.dot(ch, hi, preferred_element_type=F32) + jnp.dot(
            ch, lo, preferred_element_type=F32
        )
        for j in range(TILES // parts):
            d = p * (TILES // parts) + j
            for f in range(F):
                slab[d * MSG + f * 8:d * MSG + f * 8 + 8, :] = packed[
                    j * 8:(j + 1) * 8, f * 128:(f + 1) * 128
                ]

        @pl.loop(max(1, p * (TILES // parts)), (p + 1) * (TILES // parts))
        def _(d):
            a2a(d).start()

    for d in ve_load:
        d.wait()
    inv[0, 0] = jnp.ones((8, 128), F32)
    inv[0, 1] = jnp.zeros((8, 128), F32)
    one, zero = inv[0, 0], inv[0, 1]
    wets = [wet[c] for c in range(CB)]

    def factor(i, carry):
        e_t, e_b, _, r_g = carry
        n_t, n_b, n_g = [], [], []
        for c in range(CB):
            a_t = ve[c, i] * wets[c]
            a_b = ve[c, LEV - 2 - i] * wets[c]
            i_t = 1.0 / (e_t[c] + a_t)
            i_b = 1.0 / (e_b[c] + a_b)
            w_t, w_b = a_t * i_t, a_b * i_b
            inv[c, i] = i_t
            inv[c, LEV - 1 - i] = i_b
            ww[c, i] = w_t
            ww[c, LEV - 1 - i] = w_b
            rg[c, i] = r_g[c]
            n_t.append(1.0 + w_t * e_t[c])
            n_b.append(1.0 + w_b * e_b[c])
            n_g.append(w_t * r_g[c])
        return n_t, n_b, e_b, n_g

    ones = [one] * CB
    zeros = [zero] * CB
    e_t, _, e_b, r_g = lax.fori_loop(0, HALF, factor, (ones, ones, ones, ones), unroll=2)
    mids = [1.0 / (e_t[c] + e_b[c] - 1.0) for c in range(CB)]
    for c in range(CB):
        mid[c] = mids[c]

    for d in edge:
        d.wait_recv()
    lane8 = iota((8, 128), 1)
    keep_above = jnp.where((dev != 0) & (dev != 96), 1.0, 0.0)
    keep_below = jnp.where((dev != 127) & (dev != 95), 1.0, 0.0)

    def neighbours(x, up, dn):
        ls = [pltpu.roll(x[c], 1, 1) for c in range(CB)]
        rs = [pltpu.roll(x[c], 127, 1) for c in range(CB)]
        out = []
        for c in range(CB):
            left = ls[c] if c == 0 else jnp.where(lane8 == 0, ls[c - 1], ls[c])
            right = rs[c] if c == CB - 1 else jnp.where(lane8 == 127, rs[c + 1], rs[c])
            above = jnp.where(row8 == 0, up[c], pltpu.roll(x[c], 1, 0))
            below = jnp.where(row8 == 7, dn[c], pltpu.roll(x[c], 7, 0))
            out.append((left, right, above, below))
        return out

    wet_up = [re[1, c, LEV + 7:LEV + 8, :] for c in range(CB)]
    wet_dn = [re[0, c, LEV:LEV + 1, :] for c in range(CB)]
    around = neighbours(
        wets, [w * keep_above for w in wet_up], [w * keep_below for w in wet_dn]
    )
    for c in range(CB):
        left, right, above, below = around[c]
        if c == 0:
            left = jnp.where(lane8 == 0, 0.0, left)
        if c == CB - 1:
            right = jnp.where(lane8 == 127, 0.0, right)
        scale = nu[:, c * 128:(c + 1) * 128] * wets[c]
        cs = [scale * v for v in (left, right, above, below)]
        for j in range(4):
            coef[j, c] = cs[j]
        coef[4, c] = 1.0 - (cs[0] + cs[1] + cs[2] + cs[3])

    def spread(x, up, dn):
        out = []
        for c, near in enumerate(neighbours(x, up, dn)):
            total = coef[4, c] * x[c]
            for j in range(4):
                total = total + coef[j, c] * near[j]
            out.append(total)
        return out

    def halo_rows(ref, l):
        return [ref[c, pl.ds(l, 1), :] for c in range(CB)]

    def first(i, carry):
        r_t, r_b = carry
        l_t, l_b = i, LEV - 1 - i
        h_t = spread([st[c, l_t] for c in range(CB)], halo_rows(re.at[1], l_t), halo_rows(re.at[0], l_t))
        h_b = spread([st[c, l_b] for c in range(CB)], halo_rows(re.at[1], l_b), halo_rows(re.at[0], l_b))
        n_t, n_b = [], []
        for c in range(CB):
            r = h_t[c] + r_t[c]
            s = h_b[c] + r_b[c]
            ru_fwd[c, l_t] = r
            ru_fwd[c, l_b] = s
            n_t.append(ww[c, l_t] * r)
            n_b.append(ww[c, l_b] * s)
        return n_t, n_b

    r_t, _ = lax.fori_loop(0, HALF, first, (zeros, zeros))
    x_b, x_t, y_b, y_t = [], [], [], []
    for c in range(CB):
        x32 = (ru_fwd[c, HALF] + r_t[c]) * mids[c]
        y32 = r_g[c] * mids[c]
        x_t.append(x32)
        y_t.append(y32)
        x_b.append(inv[c, HALF - 1] * ru_fwd[c, HALF - 1] + ww[c, HALF - 1] * x32)
        y_b.append(inv[c, HALF - 1] * rg[c, HALF - 1] + ww[c, HALF - 1] * y32)

    def back(i, carry):
        x_t, x_b, y_t, y_b = carry
        l_t, l_b = HALF - 1 - i, HALF + i
        n = [[], [], [], []]
        for c in range(CB):
            w_t, w_b, i_t, i_b = ww[c, l_t], ww[c, l_b], inv[c, l_t], inv[c, l_b]
            x0 = i_t * ru_fwd[c, l_t] + w_t * x_t[c]
            x1 = i_b * ru_fwd[c, l_b] + w_b * x_b[c]
            y0 = i_t * rg[c, l_t] + w_t * y_t[c]
            y1 = w_b * y_b[c]
            uu[c, l_t] = x0
            uu[c, l_b] = x1
            gg[c, l_t] = y0
            gg[c, l_b] = y1
            for a, v in zip(n, (x0, x1, y0, y1)):
                a.append(v)
        return tuple(n)

    lax.fori_loop(0, HALF, back, (x_t, x_b, y_t, y_b), unroll=2)

    for c in range(CB):
        rows_u = uu.at[c].reshape(LEV * 8, 128)
        rows_g = gg.at[c].reshape(LEV * 8, 128)
        for side in range(2):
            su[side, 0, c] = rows_u[pl.ds(7 * side, LEV, stride=8), :]
            su[side, 1, c] = rows_g[pl.ds(7 * side, LEV, stride=8), :]
    edge_u = [halo(su, ru, side, 1) for side in range(2)]
    for d in edge_u:
        d.start()

    got[0:MSG, :] = slab[0:MSG, :]

    @pl.loop(1, TILES)
    def _(d):
        a2a(d).wait_recv()

    halves = []
    for h in range(2):
        t = got[pl.ds(h * 16 * MSG + 32, 8, stride=MSG), :] + got[
            pl.ds((h * 16 + 8) * MSG + 32, 8, stride=MSG), :
        ]
        halves.append(jnp.sum(t, axis=0, keepdims=True))
    tag_row = jnp.concatenate(halves, axis=1)
    m = iota((96, 256), 0)
    want = (m // 32) * 32 + (m % 8) * 4 + (m % 32) // 8 + 1
    ch2 = one_hot(want.astype(F32) == tag_row)
    for f in range(F):
        items = jnp.concatenate(
            [got[d * MSG + f * 8:d * MSG + f * 8 + 8, :] for d in range(TILES)], axis=0
        )
        hi, lo = split(items)
        part = jnp.dot(ch2, hi, preferred_element_type=F32) + jnp.dot(
            ch2, lo, preferred_element_type=F32
        )
        for g in range(3):
            for c in range(CB):
                ps[g, c, f] = part[g * 32 + c * 8:g * 32 + c * 8 + 8]
    for g in range(3):
        for c in range(CB):
            tot = ps[g, c, 0] + ps[g, c, 1] + ps[g, c, 2] + ps[g, c, 3]
            es[g, 0, c:c + 1, :] = tot[0:1]
            es[g, 1, c:c + 1, :] = tot[7:8]

    def across(g, src, to, j):
        return pltpu.make_async_remote_copy(
            src_ref=src, dst_ref=xr.at[j], send_sem=xss.at[g], recv_sem=xrs.at[j],
            device_id=to, device_id_type=MESH,
        )

    def across_edge(g, side, to, j):
        return pltpu.make_async_remote_copy(
            src_ref=es.at[g, side], dst_ref=xe.at[j, side], send_sem=ess.at[g, side],
            recv_sem=ers.at[j, side], device_id=to, device_id_type=MESH,
        )

    def ocean_sends():
        copies = []
        for g in range(3):
            copies.append(across_edge(g, 0, dev_id((g * TILES + tile + 95) % 96), 0))
            copies.append(across_edge(g, 1, dev_id((g * TILES + tile + 1) % 96), 0))
            copies.append(across(g, ps.at[g], (g, tile), 0))
        return copies

    def air_sends():
        return [
            across_edge(0, 0, (3, t_prev), grp),
            across_edge(0, 1, (3, t_next), grp),
            across(0, ps.at[0], (3, tile), grp),
        ]

    @pl.when(ocean)
    def _():
        for d in ocean_sends():
            d.start()
        for j in range(3):
            across(j, ps.at[0], (0, tile), j).wait_recv()
            for side in range(2):
                across_edge(j, side, (0, tile), j).wait_recv()

    @pl.when(jnp.logical_not(ocean))
    def _():
        for d in air_sends():
            d.start()
        for j in range(1, 3):
            xr[j] = jnp.zeros(xr.shape[1:], F32)
            xe[j] = jnp.zeros(xe.shape[1:], F32)
        across(0, ps.at[0], (3, tile), 0).wait_recv()
        for side in range(2):
            across_edge(0, side, (3, tile), 0).wait_recv()

    forc, f_up, f_dn = [], [], []
    e_up = (xe[0, 1] + xe[1, 1] + xe[2, 1]) * GAIN
    e_dn = (xe[0, 0] + xe[1, 0] + xe[2, 0]) * GAIN
    for c in range(CB):
        tot = None
        for f in range(F):
            r = xr[0, c, f] + xr[1, c, f] + xr[2, c, f]
            rv[c, f] = r
            tot = r if tot is None else tot + r
        forc.append(GAIN * wets[c] * tot)
        f_up.append(e_up[c:c + 1] * wet_up[c])
        f_dn.append(e_dn[c:c + 1] * wet_dn[c])
    rec_out = [
        pltpu.make_async_copy(rv.at[c], rec_h.at[:, :, c * 128:(c + 1) * 128], lsem.at[c])
        for c in range(CB)
    ]
    for d in rec_out:
        d.start()

    for d in edge_u:
        d.wait_recv()

    def level(l):
        x = [uu[c, l] + gg[c, l] * forc[c] for c in range(CB)]
        up = [
            ru[1, 0, c, pl.ds(l, 1), :] + ru[1, 1, c, pl.ds(l, 1), :] * f_up[c] for c in range(CB)
        ]
        dn = [
            ru[0, 0, c, pl.ds(l, 1), :] + ru[0, 1, c, pl.ds(l, 1), :] * f_dn[c] for c in range(CB)
        ]
        return spread(x, up, dn)

    def second(i, carry):
        r_t, r_b = carry
        l_t, l_b = i, LEV - 1 - i
        h_t, h_b = level(l_t), level(l_b)
        n_t, n_b = [], []
        for c in range(CB):
            r = h_t[c] + r_t[c]
            s = h_b[c] + r_b[c]
            ru_fwd[c, l_t] = r
            ru_fwd[c, l_b] = s
            n_t.append(ww[c, l_t] * r)
            n_b.append(ww[c, l_b] * s)
        return n_t, n_b

    r_t, _ = lax.fori_loop(0, HALF, second, (forc, zeros))
    x_t, x_b = [], []
    for c in range(CB):
        x32 = (ru_fwd[c, HALF] + r_t[c]) * mid[c]
        x_t.append(x32)
        x_b.append(inv[c, HALF - 1] * ru_fwd[c, HALF - 1] + ww[c, HALF - 1] * x32)

    def back2(i, carry):
        x_t, x_b = carry
        l_t, l_b = HALF - 1 - i, HALF + i
        n_t, n_b = [], []
        for c in range(CB):
            x0 = inv[c, l_t] * ru_fwd[c, l_t] + ww[c, l_t] * x_t[c]
            x1 = inv[c, l_b] * ru_fwd[c, l_b] + ww[c, l_b] * x_b[c]
            outv[c, l_t] = x0
            outv[c, l_b] = x1
            n_t.append(x0)
            n_b.append(x1)
        return n_t, n_b

    lax.fori_loop(0, HALF, back2, (x_t, x_b), unroll=2)
    st_out = [
        pltpu.make_async_copy(outv.at[c], out_h.at[:, :, c * 128:(c + 1) * 128], lsem.at[4 + c])
        for c in range(CB)
    ]
    for d in st_out:
        d.start()

    for d in edge + edge_u:
        d.wait_send()

    @pl.loop(1, TILES)
    def _(d):
        a2a(d).wait_send()

    @pl.when(ocean)
    def _():
        for d in ocean_sends():
            d.wait_send()

    @pl.when(jnp.logical_not(ocean))
    def _():
        for d in air_sends():
            d.wait_send()

    for d in st_out + rec_out:
        d.wait()


def local(*args):
    vm = pltpu.VMEM
    dma = pltpu.SemaphoreType.DMA
    col = (CB, LEV, 8, 128)
    scratch = [
        vm((32, K, 128, 128), BF16), vm(col, F32), vm((CB, LEV - 1, 8, 128), F32),
        vm((8, 512), F32), vm((8, 512), jnp.int32), vm((F, 8, 512), F32), vm((F, 8, 512), F32),
        vm((32, K), jnp.int32), vm((32, K), jnp.int32), vm((32, K), jnp.int32),
        vm((128, 128), F32), vm((512, 128), F32),
        vm((TILES * MSG, 128), F32), vm((TILES * MSG, 128), F32),
        vm((3, CB, F, 8, 128), F32), vm((3, CB, F, 8, 128), F32),
        vm((3, 2, 8, 128), F32), vm((3, 2, 8, 128), F32),
        vm((2, CB, LEV + 8, 128), F32), vm((2, CB, LEV + 8, 128), F32),
        vm((2, 2, CB, LEV, 128), F32), vm((2, 2, CB, LEV, 128), F32),
        vm((5, CB, 8, 128), F32), vm((CB, 8, 128), F32),
        vm(col, F32), vm(col, F32), vm((CB, 8, 128), F32),
        vm((CB, HALF, 8, 128), F32), vm(col, F32), vm(col, F32), vm(col, F32), vm(col, F32),
        vm((CB, F, 8, 128), F32),
        dma((15,)), dma((WCH,)), dma((TILES,)), dma((TILES,)), dma((2, 2)), dma((2, 2)),
        dma((3,)), dma((3,)), dma((3, 2)), dma((3, 2)),
    ]
    any_spec = pl.BlockSpec(memory_space=pl.ANY)
    return pl.pallas_call(
        kernel,
        out_shape=(
            jax.ShapeDtypeStruct((LEV, 8, 512), F32), jax.ShapeDtypeStruct((F, 8, 512), F32),
        ),
        in_specs=[any_spec] * 10,
        out_specs=(any_spec, any_spec),
        scratch_shapes=scratch,
        compiler_params=pltpu.CompilerParams(
            collective_id=0, has_side_effects=True, vmem_limit_bytes=50 * 1024 * 1024
        ),
        name="window",
    )(*args)


def solution(mesh):
    both = ("grp", "tile")
    in_specs = (
        P(None, both, None), P(None, both, None), P(both, None), P("tile", None),
        P(None, both, None), P(None, both, None), P(both, None, None, None),
        P(both, None), P(both, None), P(both, None),
    )
    out_specs = (P(None, both, None), P(None, both, None))
    return jax.shard_map(local, mesh=mesh, in_specs=in_specs, out_specs=out_specs, check_vma=False)
```

```python
import functools

import jax
import jax.numpy as jnp
from jax import lax
from jax.experimental import pallas as pl
from jax.experimental.pallas import tpu as pltpu
from jax.sharding import PartitionSpec as P

MESH = pl.DeviceIdType.MESH
F32 = jnp.float32
BF16 = jnp.bfloat16
F = 4
K = 4
LEV = 64
HALF = LEV // 2
TILES = 32
SLOTS = 8
MSG = 40
CB = 4
WCH = 8
GAIN = 0.25


def iota(shape, dim):
    return lax.broadcasted_iota(jnp.int32, shape, dim)


def one_hot(mask):
    return jnp.where(mask, 1.0, 0.0).astype(BF16)


def split(x):
    hi = x.astype(BF16)
    return hi, (x - hi.astype(F32)).astype(BF16)


def kernel(
    state_h, vert_h, nu_h, mask_h, coup_h, surf_h, w_h, dt_h, db_h, dg_h,
    out_h, rec_h,
    w_v, st, ve, nu, mask, coup, surf, dt, db, dg,
    xs, terms, slab, got, ps, xr, es, xe,
    se, re, su, ru, coef, wet, inv, ww, mid, rg, ru_fwd, uu, gg,
    lsem, wsem, ssem, rsem, hs, hr, xss, xrs, ess, ers,
):
    grp = lax.axis_index("grp")
    tile = lax.axis_index("tile")
    dev = grp * TILES + tile
    ocean = grp == 3
    n_dev = 4 * TILES

    def dev_id(flat):
        return (flat // TILES, flat % TILES)

    above_dev = dev_id((dev + n_dev - 1) % n_dev)
    below_dev = dev_id((dev + 1) % n_dev)
    t_prev, t_next = (tile + TILES - 1) % TILES, (tile + 1) % TILES

    def load(src, dst, i):
        return pltpu.make_async_copy(src, dst, lsem.at[i])

    small = [
        load(dt_h, dt, 0), load(db_h, db, 1), load(dg_h, dg, 2),
        load(mask_h, mask, 3), load(coup_h, coup, 4), load(surf_h, surf, 5), load(nu_h, nu, 6),
    ]
    st_load = [load(state_h.at[:, :, c * 128:(c + 1) * 128], st.at[c], 7 + c) for c in range(CB)]
    ve_load = [
        load(vert_h.at[:, :, c * 128:(c + 1) * 128], ve.at[c], 11 + c) for c in range(CB)
    ]
    per = 32 // WCH
    w_load = [
        pltpu.make_async_copy(w_h.at[pl.ds(i * per, per)], w_v.at[pl.ds(i * per, per)], wsem.at[i])
        for i in range(WCH)
    ]
    for d in small + st_load + w_load + ve_load:
        d.start()

    barrier = pltpu.get_barrier_semaphore()

    def tell(device):
        pl.semaphore_signal(barrier, inc=1, device_id=device, device_id_type=MESH)

    @pl.loop(1, TILES)
    def _(d):
        tell((grp, (tile + d) % TILES))

    tell(above_dev)
    tell(below_dev)

    @pl.when(ocean)
    def _():
        for g in range(3):
            for t in (tile, t_prev, t_next):
                tell((g, t))

    @pl.when(jnp.logical_not(ocean))
    def _():
        for t in (tile, t_prev, t_next):
            tell((3, t))

    for d in small:
        d.wait()

    lane = iota((1, 128), 1)
    k_of = lane % 4
    b_of = 2 * ((lane % 64) // 4) + lane // 64
    group_label = jnp.where(ocean, 32, 0)
    both = jnp.concatenate(
        [((dt[...] + TILES - tile) % TILES).astype(F32),
         (db[...] + dg[...] * group_label + 1).astype(F32)], axis=0
    ).astype(BF16)
    wide = jnp.dot(both, one_hot(iota((32, 128), 0) == b_of), preferred_element_type=F32)
    of_k = iota((K, 128), 0) == k_of
    d_row = jnp.sum(jnp.where(of_k, wide[:K], 0.0), axis=0, keepdims=True)
    label = jnp.sum(jnp.where(of_k, wide[K:], 0.0), axis=0, keepdims=True)
    drel = d_row.astype(jnp.int32)
    i0, i1 = iota((128, 128), 0), iota((128, 128), 1)
    d_col = jnp.sum(jnp.where(i0 == i1, d_row, 0.0), axis=1, keepdims=True)
    pos = jnp.sum(jnp.where((d_col == d_row) & (i0 < i1), 1.0, 0.0), axis=0, keepdims=True)
    slot = drel * SLOTS + pos.astype(jnp.int32)
    tag_a = jnp.where(iota((TILES, 128), 0) == drel, label, 0.0).astype(BF16)
    tag_b = one_hot(i0 == slot % 128)
    tags = lax.dot_general(tag_a, tag_b, (((1,), (1,)), ((), ())), preferred_element_type=F32)
    for j in range(TILES // 8):
        slab[pl.ds(j * 8 * MSG + 32, 8, stride=MSG), :] = tags[j * 8:(j + 1) * 8]

    for d in st_load:
        d.wait()
    for c in range(CB):
        cs = slice(c * 128, (c + 1) * 128)
        wet_c = jnp.where(ocean, mask[:, cs].astype(F32), 1.0)
        wet[c] = wet_c
        for f in range(F):
            send = coup[f, :, cs] * (st[c, 0] - surf[f, :, cs]) * wet_c
            xs[pl.ds(c * 4 + f, 8, stride=16), :] = send

    for c in range(CB):
        rows = st.at[c].reshape(LEV * 8, 128)
        for side in range(2):
            se[side, c, 0:LEV, :] = rows[pl.ds(7 * side, LEV, stride=8), :]
            se[side, c, LEV:LEV + 8, :] = wet[c]

    @pl.when(ocean)
    def _():
        pl.semaphore_wait(barrier, 31 + 2 + 9)

    @pl.when(jnp.logical_not(ocean))
    def _():
        pl.semaphore_wait(barrier, 31 + 2 + 3)

    def halo(src, dst, side, i):
        return pltpu.make_async_remote_copy(
            src_ref=src.at[side], dst_ref=dst.at[side], send_sem=hs.at[i, side],
            recv_sem=hr.at[i, side], device_id=above_dev if side == 0 else below_dev,
            device_id_type=MESH,
        )

    edge = [halo(se, re, side, 0) for side in range(2)]
    for d in edge:
        d.start()

    row8 = iota((8, 128), 0)

    def two_blocks(q):
        x8 = xs[pl.ds(q * 8, 8), :]
        x = jnp.concatenate(
            [jnp.where(row8 < 4, x8, 0.0), jnp.where(row8 < 4, 0.0, x8)], axis=1
        ).astype(BF16)
        for kp in range(2):
            cols = [w_v[pl.ds(2 * q, 2), 2 * kp + j].reshape(256, 128) for j in range(2)]
            t = jnp.dot(x, jnp.concatenate(cols, axis=1), preferred_element_type=F32)
            for j in range(2):
                terms[pl.ds(q * 4 + 2 * kp + j, 8, stride=64), :] = t[:, j * 128:(j + 1) * 128]

    for i in range(WCH):
        w_load[i].wait()
        for q in range(i * 16 // WCH, (i + 1) * 16 // WCH):
            two_blocks(q)

    his, los = [], []
    for f in range(F):
        t = jnp.concatenate([terms[bl * 256 + f * 64:bl * 256 + f * 64 + 64, :] for bl in range(2)], 0)
        hi, lo = split(t)
        his.append(hi)
        los.append(lo)
    hi = jnp.concatenate(his, axis=1)
    lo = jnp.concatenate(los, axis=1)

    def a2a(d):
        return pltpu.make_async_remote_copy(
            src_ref=slab.at[pl.ds(d * MSG, MSG)], dst_ref=got.at[pl.ds(d * MSG, MSG)],
            send_sem=ssem.at[d], recv_sem=rsem.at[d],
            device_id=(grp, (tile + d) % TILES), device_id_type=MESH,
        )

    parts = 4
    rows = TILES * SLOTS // parts
    for p in range(parts):
        ch = one_hot(iota((rows, 128), 0) + p * rows == slot)
        packed = jnp.dot(ch, hi, preferred_element_type=F32) + jnp.dot(
            ch, lo, preferred_element_type=F32
        )
        for j in range(TILES // parts):
            d = p * (TILES // parts) + j
            for f in range(F):
                slab[d * MSG + f * 8:d * MSG + f * 8 + 8, :] = packed[
                    j * 8:(j + 1) * 8, f * 128:(f + 1) * 128
                ]

        @pl.loop(max(1, p * (TILES // parts)), (p + 1) * (TILES // parts))
        def _(d):
            a2a(d).start()

    for d in ve_load:
        d.wait()
    inv[0, 0] = jnp.ones((8, 128), F32)
    inv[0, 1] = jnp.zeros((8, 128), F32)
    one, zero = inv[0, 0], inv[0, 1]
    wets = [wet[c] for c in range(CB)]

    def factor(i, carry):
        e_t, e_b, _, r_g = carry
        n_t, n_b, n_g = [], [], []
        for c in range(CB):
            a_t = ve[c, i] * wets[c]
            a_b = ve[c, LEV - 2 - i] * wets[c]
            i_t = 1.0 / (e_t[c] + a_t)
            i_b = 1.0 / (e_b[c] + a_b)
            w_t, w_b = a_t * i_t, a_b * i_b
            inv[c, i] = i_t
            inv[c, LEV - 1 - i] = i_b
            ww[c, i] = w_t
            ww[c, LEV - 1 - i] = w_b
            rg[c, i] = r_g[c]
            n_t.append(1.0 + w_t * e_t[c])
            n_b.append(1.0 + w_b * e_b[c])
            n_g.append(w_t * r_g[c])
        return n_t, n_b, e_b, n_g

    ones = [one] * CB
    zeros = [zero] * CB
    e_t, _, e_b, r_g = lax.fori_loop(0, HALF, factor, (ones, ones, ones, ones), unroll=2)
    mids = [1.0 / (e_t[c] + e_b[c] - 1.0) for c in range(CB)]
    for c in range(CB):
        mid[c] = mids[c]

    for d in edge:
        d.wait_recv()
    lane8 = iota((8, 128), 1)
    keep_above = jnp.where((dev != 0) & (dev != 96), 1.0, 0.0)
    keep_below = jnp.where((dev != 127) & (dev != 95), 1.0, 0.0)

    def neighbours(x, up, dn):
        ls = [pltpu.roll(x[c], 1, 1) for c in range(CB)]
        rs = [pltpu.roll(x[c], 127, 1) for c in range(CB)]
        out = []
        for c in range(CB):
            left = ls[c] if c == 0 else jnp.where(lane8 == 0, ls[c - 1], ls[c])
            right = rs[c] if c == CB - 1 else jnp.where(lane8 == 127, rs[c + 1], rs[c])
            above = jnp.where(row8 == 0, up[c], pltpu.roll(x[c], 1, 0))
            below = jnp.where(row8 == 7, dn[c], pltpu.roll(x[c], 7, 0))
            out.append((left, right, above, below))
        return out

    wet_up = [re[1, c, LEV + 7:LEV + 8, :] for c in range(CB)]
    wet_dn = [re[0, c, LEV:LEV + 1, :] for c in range(CB)]
    around = neighbours(
        wets, [w * keep_above for w in wet_up], [w * keep_below for w in wet_dn]
    )
    for c in range(CB):
        left, right, above, below = around[c]
        if c == 0:
            left = jnp.where(lane8 == 0, 0.0, left)
        if c == CB - 1:
            right = jnp.where(lane8 == 127, 0.0, right)
        scale = nu[:, c * 128:(c + 1) * 128] * wets[c]
        cs = [scale * v for v in (left, right, above, below)]
        for j in range(4):
            coef[j, c] = cs[j]
        coef[4, c] = 1.0 - (cs[0] + cs[1] + cs[2] + cs[3])

    def spread(x, up, dn):
        out = []
        for c, near in enumerate(neighbours(x, up, dn)):
            total = coef[4, c] * x[c]
            for j in range(4):
                total = total + coef[j, c] * near[j]
            out.append(total)
        return out

    def halo_rows(ref, l):
        return [ref[c, pl.ds(l, 1), :] for c in range(CB)]

    def first(i, carry):
        r_t, r_b = carry
        l_t, l_b = i, LEV - 1 - i
        h_t = spread([st[c, l_t] for c in range(CB)], halo_rows(re.at[1], l_t), halo_rows(re.at[0], l_t))
        h_b = spread([st[c, l_b] for c in range(CB)], halo_rows(re.at[1], l_b), halo_rows(re.at[0], l_b))
        n_t, n_b = [], []
        for c in range(CB):
            r = h_t[c] + r_t[c]
            s = h_b[c] + r_b[c]
            ru_fwd[c, l_t] = r
            ru_fwd[c, l_b] = s
            n_t.append(ww[c, l_t] * r)
            n_b.append(ww[c, l_b] * s)
        return n_t, n_b

    r_t, _ = lax.fori_loop(0, HALF, first, (zeros, zeros))
    x_b, x_t, y_b, y_t = [], [], [], []
    for c in range(CB):
        x32 = (ru_fwd[c, HALF] + r_t[c]) * mids[c]
        y32 = r_g[c] * mids[c]
        x_t.append(x32)
        y_t.append(y32)
        x_b.append(inv[c, HALF - 1] * ru_fwd[c, HALF - 1] + ww[c, HALF - 1] * x32)
        y_b.append(inv[c, HALF - 1] * rg[c, HALF - 1] + ww[c, HALF - 1] * y32)

    def back(i, carry):
        x_t, x_b, y_t, y_b = carry
        l_t, l_b = HALF - 1 - i, HALF + i
        n = [[], [], [], []]
        for c in range(CB):
            w_t, w_b, i_t, i_b = ww[c, l_t], ww[c, l_b], inv[c, l_t], inv[c, l_b]
            x0 = i_t * ru_fwd[c, l_t] + w_t * x_t[c]
            x1 = i_b * ru_fwd[c, l_b] + w_b * x_b[c]
            y0 = i_t * rg[c, l_t] + w_t * y_t[c]
            y1 = w_b * y_b[c]
            uu[c, l_t] = x0
            uu[c, l_b] = x1
            gg[c, l_t] = y0
            gg[c, l_b] = y1
            for a, v in zip(n, (x0, x1, y0, y1)):
                a.append(v)
        return tuple(n)

    lax.fori_loop(0, HALF, back, (x_t, x_b, y_t, y_b), unroll=2)

    for c in range(CB):
        rows_u = uu.at[c].reshape(LEV * 8, 128)
        rows_g = gg.at[c].reshape(LEV * 8, 128)
        for side in range(2):
            su[side, 0, c] = rows_u[pl.ds(7 * side, LEV, stride=8), :]
            su[side, 1, c] = rows_g[pl.ds(7 * side, LEV, stride=8), :]
    edge_u = [halo(su, ru, side, 1) for side in range(2)]
    for d in edge_u:
        d.start()

    got[0:MSG, :] = slab[0:MSG, :]

    @pl.loop(1, TILES)
    def _(d):
        a2a(d).wait_recv()

    halves = []
    for h in range(2):
        t = got[pl.ds(h * 16 * MSG + 32, 8, stride=MSG), :] + got[
            pl.ds((h * 16 + 8) * MSG + 32, 8, stride=MSG), :
        ]
        halves.append(jnp.sum(t, axis=0, keepdims=True))
    tag_row = jnp.concatenate(halves, axis=1)
    m = iota((96, 256), 0)
    want = (m // 32) * 32 + (m % 8) * 4 + (m % 32) // 8 + 1
    ch2 = one_hot(want.astype(F32) == tag_row)
    for f in range(F):
        items = jnp.concatenate(
            [got[d * MSG + f * 8:d * MSG + f * 8 + 8, :] for d in range(TILES)], axis=0
        )
        hi, lo = split(items)
        part = jnp.dot(ch2, hi, preferred_element_type=F32) + jnp.dot(
            ch2, lo, preferred_element_type=F32
        )
        for g in range(3):
            for c in range(CB):
                ps[g, c, f] = part[g * 32 + c * 8:g * 32 + c * 8 + 8]
    for g in range(3):
        for c in range(CB):
            tot = ps[g, c, 0] + ps[g, c, 1] + ps[g, c, 2] + ps[g, c, 3]
            es[g, 0, c:c + 1, :] = tot[0:1]
            es[g, 1, c:c + 1, :] = tot[7:8]

    def across(g, src, to, j):
        return pltpu.make_async_remote_copy(
            src_ref=src, dst_ref=xr.at[j], send_sem=xss.at[g], recv_sem=xrs.at[j],
            device_id=to, device_id_type=MESH,
        )

    def across_edge(g, side, to, j):
        return pltpu.make_async_remote_copy(
            src_ref=es.at[g, side], dst_ref=xe.at[j, side], send_sem=ess.at[g, side],
            recv_sem=ers.at[j, side], device_id=to, device_id_type=MESH,
        )

    def ocean_sends():
        copies = []
        for g in range(3):
            copies.append(across_edge(g, 0, dev_id((g * TILES + tile + 95) % 96), 0))
            copies.append(across_edge(g, 1, dev_id((g * TILES + tile + 1) % 96), 0))
            copies.append(across(g, ps.at[g], (g, tile), 0))
        return copies

    def air_sends():
        return [
            across_edge(0, 0, (3, t_prev), grp),
            across_edge(0, 1, (3, t_next), grp),
            across(0, ps.at[0], (3, tile), grp),
        ]

    @pl.when(ocean)
    def _():
        for d in ocean_sends():
            d.start()
        for j in range(3):
            across(j, ps.at[0], (0, tile), j).wait_recv()
            for side in range(2):
                across_edge(j, side, (0, tile), j).wait_recv()

    @pl.when(jnp.logical_not(ocean))
    def _():
        for d in air_sends():
            d.start()
        for j in range(1, 3):
            xr[j] = jnp.zeros(xr.shape[1:], F32)
            xe[j] = jnp.zeros(xe.shape[1:], F32)
        across(0, ps.at[0], (3, tile), 0).wait_recv()
        for side in range(2):
            across_edge(0, side, (3, tile), 0).wait_recv()

    forc, f_up, f_dn = [], [], []
    e_up = (xe[0, 1] + xe[1, 1] + xe[2, 1]) * GAIN
    e_dn = (xe[0, 0] + xe[1, 0] + xe[2, 0]) * GAIN
    for c in range(CB):
        tot = None
        for f in range(F):
            r = xr[0, c, f] + xr[1, c, f] + xr[2, c, f]
            rec_h[f, :, c * 128:(c + 1) * 128] = r
            tot = r if tot is None else tot + r
        forc.append(GAIN * wets[c] * tot)
        f_up.append(e_up[c:c + 1] * wet_up[c])
        f_dn.append(e_dn[c:c + 1] * wet_dn[c])
    for d in edge_u:
        d.wait_recv()

    def level(l):
        x = [uu[c, l] + gg[c, l] * forc[c] for c in range(CB)]
        up = [
            ru[1, 0, c, pl.ds(l, 1), :] + ru[1, 1, c, pl.ds(l, 1), :] * f_up[c] for c in range(CB)
        ]
        dn = [
            ru[0, 0, c, pl.ds(l, 1), :] + ru[0, 1, c, pl.ds(l, 1), :] * f_dn[c] for c in range(CB)
        ]
        return spread(x, up, dn)

    def second(i, carry):
        r_t, r_b = carry
        l_t, l_b = i, LEV - 1 - i
        h_t, h_b = level(l_t), level(l_b)
        n_t, n_b = [], []
        for c in range(CB):
            r = h_t[c] + r_t[c]
            s = h_b[c] + r_b[c]
            ru_fwd[c, l_t] = r
            ru_fwd[c, l_b] = s
            n_t.append(ww[c, l_t] * r)
            n_b.append(ww[c, l_b] * s)
        return n_t, n_b

    r_t, _ = lax.fori_loop(0, HALF, second, (forc, zeros))
    x_t, x_b = [], []
    for c in range(CB):
        x32 = (ru_fwd[c, HALF] + r_t[c]) * mid[c]
        x_t.append(x32)
        x_b.append(inv[c, HALF - 1] * ru_fwd[c, HALF - 1] + ww[c, HALF - 1] * x32)

    def back2(i, carry):
        x_t, x_b = carry
        l_t, l_b = HALF - 1 - i, HALF + i
        n_t, n_b = [], []
        for c in range(CB):
            x0 = inv[c, l_t] * ru_fwd[c, l_t] + ww[c, l_t] * x_t[c]
            x1 = inv[c, l_b] * ru_fwd[c, l_b] + ww[c, l_b] * x_b[c]
            out_h[l_t, :, c * 128:(c + 1) * 128] = x0
            out_h[l_b, :, c * 128:(c + 1) * 128] = x1
            n_t.append(x0)
            n_b.append(x1)
        return n_t, n_b

    lax.fori_loop(0, HALF, back2, (x_t, x_b), unroll=2)
    for d in edge + edge_u:
        d.wait_send()

    @pl.loop(1, TILES)
    def _(d):
        a2a(d).wait_send()

    @pl.when(ocean)
    def _():
        for d in ocean_sends():
            d.wait_send()

    @pl.when(jnp.logical_not(ocean))
    def _():
        for d in air_sends():
            d.wait_send()


def local(*args):
    vm = pltpu.VMEM
    dma = pltpu.SemaphoreType.DMA
    col = (CB, LEV, 8, 128)
    scratch = [
        vm((32, K, 128, 128), BF16), vm(col, F32), vm((CB, LEV - 1, 8, 128), F32),
        vm((8, 512), F32), vm((8, 512), jnp.int32), vm((F, 8, 512), F32), vm((F, 8, 512), F32),
        vm((K, 32), jnp.int32), vm((K, 32), jnp.int32), vm((K, 32), jnp.int32),
        vm((128, 128), F32), vm((512, 128), F32),
        vm((TILES * MSG, 128), F32), vm((TILES * MSG, 128), F32),
        vm((3, CB, F, 8, 128), F32), vm((3, CB, F, 8, 128), F32),
        vm((3, 2, 8, 128), F32), vm((3, 2, 8, 128), F32),
        vm((2, CB, LEV + 8, 128), F32), vm((2, CB, LEV + 8, 128), F32),
        vm((2, 2, CB, LEV, 128), F32), vm((2, 2, CB, LEV, 128), F32),
        vm((5, CB, 8, 128), F32), vm((CB, 8, 128), F32),
        vm(col, F32), vm(col, F32), vm((CB, 8, 128), F32),
        vm((CB, HALF, 8, 128), F32), vm(col, F32), vm(col, F32), vm(col, F32),
        dma((15,)), dma((WCH,)), dma((TILES,)), dma((TILES,)), dma((2, 2)), dma((2, 2)),
        dma((3,)), dma((3,)), dma((3, 2)), dma((3, 2)),
    ]
    hbm = pl.BlockSpec(memory_space=pltpu.HBM)
    out = pl.BlockSpec(memory_space=pltpu.VMEM)
    return pl.pallas_call(
        kernel,
        out_shape=(
            vm((LEV, 8, 512), F32), vm((F, 8, 512), F32),
        ),
        in_specs=[hbm] * 10,
        out_specs=(out, out),
        scratch_shapes=scratch,
        compiler_params=pltpu.CompilerParams(
            collective_id=0, has_side_effects=True, vmem_limit_bytes=50 * 1024 * 1024
        ),
        name="window",
    )(*(pltpu.with_memory_space_constraint(a, pltpu.HBM) for a in (*args[:7], *(a.T for a in args[7:]))))


def solution(mesh):
    both = ("grp", "tile")
    in_specs = (
        P(None, both, None), P(None, both, None), P(both, None), P("tile", None),
        P(None, both, None), P(None, both, None), P(both, None, None, None),
        P(both, None), P(both, None), P(both, None),
    )
    out_specs = (P(None, both, None), P(None, both, None))
    return jax.shard_map(local, mesh=mesh, in_specs=in_specs, out_specs=out_specs, check_vma=False)
```

```python
import functools

import jax
import jax.numpy as jnp
from jax import lax
from jax.experimental import pallas as pl
from jax.experimental.pallas import tpu as pltpu
from jax.sharding import PartitionSpec as P

MESH = pl.DeviceIdType.MESH
F32 = jnp.float32
BF16 = jnp.bfloat16
F = 4
K = 4
LEV = 64
HALF = LEV // 2
TILES = 32
SLOTS = 8
MSG = 40
SENT = 33
CB = 4
WCH = 8
GAIN = 0.25


def iota(shape, dim):
    return lax.broadcasted_iota(jnp.int32, shape, dim)


def one_hot(mask):
    return jnp.where(mask, 1.0, 0.0).astype(BF16)


def split(x):
    hi = x.astype(BF16)
    return hi, (x - hi.astype(F32)).astype(BF16)


def kernel(
    state_h, vert_h, nu_h, mask_h, coup_h, surf_h, w_h, dt_h, db_h, dg_h,
    out_h, rec_h,
    w_v, s0, st, ve, nu, mask, coup, surf, dt, db, dg,
    xs, terms, slab, got, ps, xr, es, xe,
    se, re, su, ru, coef, wet, inv, ww, mid, rg, ru_fwd, uu, gg,
    lsem, wsem, ssem, rsem, hs, hr, xss, xrs, ess, ers,
):
    grp = lax.axis_index("grp")
    tile = lax.axis_index("tile")
    dev = grp * TILES + tile
    ocean = grp == 3
    n_dev = 4 * TILES

    def dev_id(flat):
        return (flat // TILES, flat % TILES)

    above_dev = dev_id((dev + n_dev - 1) % n_dev)
    below_dev = dev_id((dev + 1) % n_dev)
    t_prev, t_next = (tile + TILES - 1) % TILES, (tile + 1) % TILES

    def load(src, dst, i):
        return pltpu.make_async_copy(src, dst, lsem.at[i])

    small = [
        load(dt_h, dt, 0), load(db_h, db, 1), load(dg_h, dg, 2),
        load(mask_h, mask, 3), load(coup_h, coup, 4), load(surf_h, surf, 5), load(nu_h, nu, 6),
        load(state_h.at[0], s0, 15),
    ]
    st_load = [load(state_h.at[:, :, c * 128:(c + 1) * 128], st.at[c], 7 + c) for c in range(CB)]
    ve_load = [
        load(vert_h.at[:, :, c * 128:(c + 1) * 128], ve.at[c], 11 + c) for c in range(CB)
    ]
    per = 32 // WCH
    w_load = [
        pltpu.make_async_copy(w_h.at[pl.ds(i * per, per)], w_v.at[pl.ds(i * per, per)], wsem.at[i])
        for i in range(WCH)
    ]
    for d in small + w_load + st_load + ve_load:
        d.start()

    barrier = pltpu.get_barrier_semaphore()

    def tell(device):
        pl.semaphore_signal(barrier, inc=1, device_id=device, device_id_type=MESH)

    @pl.loop(1, TILES)
    def _(d):
        tell((grp, (tile + d) % TILES))

    tell(above_dev)
    tell(below_dev)

    @pl.when(ocean)
    def _():
        for g in range(3):
            for t in (tile, t_prev, t_next):
                tell((g, t))

    @pl.when(jnp.logical_not(ocean))
    def _():
        for t in (tile, t_prev, t_next):
            tell((3, t))

    for d in small:
        d.wait()

    lane = iota((1, 128), 1)
    k_of = lane % 4
    b_of = 2 * ((lane % 64) // 4) + lane // 64
    group_label = jnp.where(ocean, 32, 0)
    both = jnp.concatenate(
        [((dt[...] + TILES - tile) % TILES).astype(F32),
         (db[...] + dg[...] * group_label + 1).astype(F32)], axis=0
    ).astype(BF16)
    wide = jnp.dot(both, one_hot(iota((32, 128), 0) == b_of), preferred_element_type=F32)
    of_k = iota((K, 128), 0) == k_of
    d_row = jnp.sum(jnp.where(of_k, wide[:K], 0.0), axis=0, keepdims=True)
    label = jnp.sum(jnp.where(of_k, wide[K:], 0.0), axis=0, keepdims=True)
    drel = d_row.astype(jnp.int32)
    i0, i1 = iota((128, 128), 0), iota((128, 128), 1)
    d_col = jnp.sum(jnp.where(i0 == i1, d_row, 0.0), axis=1, keepdims=True)
    pos = jnp.sum(jnp.where((d_col == d_row) & (i0 < i1), 1.0, 0.0), axis=0, keepdims=True)
    slot = drel * SLOTS + pos.astype(jnp.int32)
    tag_a = jnp.where(iota((TILES, 128), 0) == drel, label, 0.0).astype(BF16)
    tag_b = one_hot(i0 == slot % 128)
    tags = lax.dot_general(tag_a, tag_b, (((1,), (1,)), ((), ())), preferred_element_type=F32)
    for j in range(TILES // 8):
        slab[pl.ds(j * 8 * MSG + 32, 8, stride=MSG), :] = tags[j * 8:(j + 1) * 8]

    for c in range(CB):
        cs = slice(c * 128, (c + 1) * 128)
        wet_c = jnp.where(ocean, mask[:, cs].astype(F32), 1.0)
        wet[c] = wet_c
        for f in range(F):
            send = coup[f, :, cs] * (s0[:, cs] - surf[f, :, cs]) * wet_c
            xs[pl.ds(c * 4 + f, 8, stride=16), :] = send

    row8 = iota((8, 128), 0)

    def two_blocks(q):
        x8 = xs[pl.ds(q * 8, 8), :]
        x = jnp.concatenate(
            [jnp.where(row8 < 4, x8, 0.0), jnp.where(row8 < 4, 0.0, x8)], axis=1
        ).astype(BF16)
        for kp in range(2):
            cols = [w_v[pl.ds(2 * q, 2), 2 * kp + j].reshape(256, 128) for j in range(2)]
            t = jnp.dot(x, jnp.concatenate(cols, axis=1), preferred_element_type=F32)
            for j in range(2):
                terms[pl.ds(q * 4 + 2 * kp + j, 8, stride=64), :] = t[:, j * 128:(j + 1) * 128]

    for i in range(WCH):
        w_load[i].wait()
        for q in range(i * 16 // WCH, (i + 1) * 16 // WCH):
            two_blocks(q)

    his, los = [], []
    for f in range(F):
        t = jnp.concatenate([terms[bl * 256 + f * 64:bl * 256 + f * 64 + 64, :] for bl in range(2)], 0)
        hi, lo = split(t)
        his.append(hi)
        los.append(lo)
    hi = jnp.concatenate(his, axis=1)
    lo = jnp.concatenate(los, axis=1)

    @pl.when(ocean)
    def _():
        pl.semaphore_wait(barrier, 31 + 2 + 9)

    @pl.when(jnp.logical_not(ocean))
    def _():
        pl.semaphore_wait(barrier, 31 + 2 + 3)

    def a2a(d):
        return pltpu.make_async_remote_copy(
            src_ref=slab.at[pl.ds(d * MSG, SENT)], dst_ref=got.at[pl.ds(d * MSG, SENT)],
            send_sem=ssem.at[d], recv_sem=rsem.at[d],
            device_id=(grp, (tile + d) % TILES), device_id_type=MESH,
        )

    parts = 4
    rows = TILES * SLOTS // parts
    for p in range(parts):
        ch = one_hot(iota((rows, 128), 0) + p * rows == slot)
        packed = jnp.dot(ch, hi, preferred_element_type=F32) + jnp.dot(
            ch, lo, preferred_element_type=F32
        )
        for j in range(TILES // parts):
            d = p * (TILES // parts) + j
            for f in range(F):
                slab[d * MSG + f * 8:d * MSG + f * 8 + 8, :] = packed[
                    j * 8:(j + 1) * 8, f * 128:(f + 1) * 128
                ]

        @pl.loop(max(1, p * (TILES // parts)), (p + 1) * (TILES // parts))
        def _(d):
            a2a(d).start()

    for d in st_load:
        d.wait()
    for c in range(CB):
        rows = st.at[c].reshape(LEV * 8, 128)
        for side in range(2):
            se[side, c, 0:LEV, :] = rows[pl.ds(7 * side, LEV, stride=8), :]
            se[side, c, LEV:LEV + 8, :] = wet[c]

    def halo(src, dst, side, i):
        return pltpu.make_async_remote_copy(
            src_ref=src.at[side], dst_ref=dst.at[side], send_sem=hs.at[i, side],
            recv_sem=hr.at[i, side], device_id=above_dev if side == 0 else below_dev,
            device_id_type=MESH,
        )

    edge = [halo(se, re, side, 0) for side in range(2)]
    for d in edge:
        d.start()

    for d in ve_load:
        d.wait()
    inv[0, 0] = jnp.ones((8, 128), F32)
    inv[0, 1] = jnp.zeros((8, 128), F32)
    one, zero = inv[0, 0], inv[0, 1]
    wets = [wet[c] for c in range(CB)]

    def factor(i, carry):
        e_t, e_b, _, r_g = carry
        n_t, n_b, n_g = [], [], []
        for c in range(CB):
            a_t = ve[c, i] * wets[c]
            a_b = ve[c, LEV - 2 - i] * wets[c]
            i_t = 1.0 / (e_t[c] + a_t)
            i_b = 1.0 / (e_b[c] + a_b)
            w_t, w_b = a_t * i_t, a_b * i_b
            inv[c, i] = i_t
            inv[c, LEV - 1 - i] = i_b
            ww[c, i] = w_t
            ww[c, LEV - 1 - i] = w_b
            rg[c, i] = r_g[c]
            n_t.append(1.0 + w_t * e_t[c])
            n_b.append(1.0 + w_b * e_b[c])
            n_g.append(w_t * r_g[c])
        return n_t, n_b, e_b, n_g

    ones = [one] * CB
    zeros = [zero] * CB
    e_t, _, e_b, r_g = lax.fori_loop(0, HALF, factor, (ones, ones, ones, ones), unroll=4)
    mids = [1.0 / (e_t[c] + e_b[c] - 1.0) for c in range(CB)]
    for c in range(CB):
        mid[c] = mids[c]

    for d in edge:
        d.wait_recv()
    lane8 = iota((8, 128), 1)
    keep_above = jnp.where((dev != 0) & (dev != 96), 1.0, 0.0)
    keep_below = jnp.where((dev != 127) & (dev != 95), 1.0, 0.0)

    def neighbours(x, up, dn):
        ls = [pltpu.roll(x[c], 1, 1) for c in range(CB)]
        rs = [pltpu.roll(x[c], 127, 1) for c in range(CB)]
        out = []
        for c in range(CB):
            left = ls[c] if c == 0 else jnp.where(lane8 == 0, ls[c - 1], ls[c])
            right = rs[c] if c == CB - 1 else jnp.where(lane8 == 127, rs[c + 1], rs[c])
            above = jnp.where(row8 == 0, up[c], pltpu.roll(x[c], 1, 0))
            below = jnp.where(row8 == 7, dn[c], pltpu.roll(x[c], 7, 0))
            out.append((left, right, above, below))
        return out

    wet_up = [re[1, c, LEV + 7:LEV + 8, :] for c in range(CB)]
    wet_dn = [re[0, c, LEV:LEV + 1, :] for c in range(CB)]
    around = neighbours(
        wets, [w * keep_above for w in wet_up], [w * keep_below for w in wet_dn]
    )
    for c in range(CB):
        left, right, above, below = around[c]
        if c == 0:
            left = jnp.where(lane8 == 0, 0.0, left)
        if c == CB - 1:
            right = jnp.where(lane8 == 127, 0.0, right)
        scale = nu[:, c * 128:(c + 1) * 128] * wets[c]
        cs = [scale * v for v in (left, right, above, below)]
        for j in range(4):
            coef[j, c] = cs[j]
        coef[4, c] = 1.0 - (cs[0] + cs[1] + cs[2] + cs[3])

    def spread(x, up, dn):
        out = []
        for c, near in enumerate(neighbours(x, up, dn)):
            total = coef[4, c] * x[c]
            for j in range(4):
                total = total + coef[j, c] * near[j]
            out.append(total)
        return out

    def halo_rows(ref, l):
        return [ref[c, pl.ds(l, 1), :] for c in range(CB)]

    def first(i, carry):
        r_t, r_b = carry
        l_t, l_b = i, LEV - 1 - i
        h_t = spread([st[c, l_t] for c in range(CB)], halo_rows(re.at[1], l_t), halo_rows(re.at[0], l_t))
        h_b = spread([st[c, l_b] for c in range(CB)], halo_rows(re.at[1], l_b), halo_rows(re.at[0], l_b))
        n_t, n_b = [], []
        for c in range(CB):
            r = h_t[c] + r_t[c]
            s = h_b[c] + r_b[c]
            ru_fwd[c, l_t] = r
            ru_fwd[c, l_b] = s
            n_t.append(ww[c, l_t] * r)
            n_b.append(ww[c, l_b] * s)
        return n_t, n_b

    r_t, _ = lax.fori_loop(0, HALF, first, (zeros, zeros), unroll=4)
    x_b, x_t, y_b, y_t = [], [], [], []
    for c in range(CB):
        x32 = (ru_fwd[c, HALF] + r_t[c]) * mids[c]
        y32 = r_g[c] * mids[c]
        x_t.append(x32)
        y_t.append(y32)
        x_b.append(inv[c, HALF - 1] * ru_fwd[c, HALF - 1] + ww[c, HALF - 1] * x32)
        y_b.append(inv[c, HALF - 1] * rg[c, HALF - 1] + ww[c, HALF - 1] * y32)

    def back(i, carry):
        x_t, x_b, y_t, y_b = carry
        l_t, l_b = HALF - 1 - i, HALF + i
        n = [[], [], [], []]
        for c in range(CB):
            w_t, w_b, i_t, i_b = ww[c, l_t], ww[c, l_b], inv[c, l_t], inv[c, l_b]
            x0 = i_t * ru_fwd[c, l_t] + w_t * x_t[c]
            x1 = i_b * ru_fwd[c, l_b] + w_b * x_b[c]
            y0 = i_t * rg[c, l_t] + w_t * y_t[c]
            y1 = w_b * y_b[c]
            uu[c, l_t] = x0
            uu[c, l_b] = x1
            gg[c, l_t] = y0
            gg[c, l_b] = y1
            for a, v in zip(n, (x0, x1, y0, y1)):
                a.append(v)
        return tuple(n)

    lax.fori_loop(0, HALF, back, (x_t, x_b, y_t, y_b), unroll=4)

    for c in range(CB):
        rows_u = uu.at[c].reshape(LEV * 8, 128)
        rows_g = gg.at[c].reshape(LEV * 8, 128)
        for side in range(2):
            su[side, 0, c] = rows_u[pl.ds(7 * side, LEV, stride=8), :]
            su[side, 1, c] = rows_g[pl.ds(7 * side, LEV, stride=8), :]
    edge_u = [halo(su, ru, side, 1) for side in range(2)]
    for d in edge_u:
        d.start()

    got[0:MSG, :] = slab[0:MSG, :]

    @pl.loop(1, TILES)
    def _(d):
        a2a(d).wait_recv()

    halves = []
    for h in range(2):
        t = got[pl.ds(h * 16 * MSG + 32, 8, stride=MSG), :] + got[
            pl.ds((h * 16 + 8) * MSG + 32, 8, stride=MSG), :
        ]
        halves.append(jnp.sum(t, axis=0, keepdims=True))
    tag_row = jnp.concatenate(halves, axis=1)
    m = iota((96, 256), 0)
    want = (m // 32) * 32 + (m % 8) * 4 + (m % 32) // 8 + 1
    ch2 = one_hot(want.astype(F32) == tag_row)
    for f in range(F):
        items = jnp.concatenate(
            [got[d * MSG + f * 8:d * MSG + f * 8 + 8, :] for d in range(TILES)], axis=0
        )
        hi, lo = split(items)
        part = jnp.dot(ch2, hi, preferred_element_type=F32) + jnp.dot(
            ch2, lo, preferred_element_type=F32
        )
        for g in range(3):
            for c in range(CB):
                ps[g, c, f] = part[g * 32 + c * 8:g * 32 + c * 8 + 8]
    for g in range(3):
        for c in range(CB):
            tot = ps[g, c, 0] + ps[g, c, 1] + ps[g, c, 2] + ps[g, c, 3]
            es[g, 0, c:c + 1, :] = tot[0:1]
            es[g, 1, c:c + 1, :] = tot[7:8]

    def across(g, src, to, j):
        return pltpu.make_async_remote_copy(
            src_ref=src, dst_ref=xr.at[j], send_sem=xss.at[g], recv_sem=xrs.at[j],
            device_id=to, device_id_type=MESH,
        )

    def across_edge(g, side, to, j):
        return pltpu.make_async_remote_copy(
            src_ref=es.at[g, side], dst_ref=xe.at[j, side], send_sem=ess.at[g, side],
            recv_sem=ers.at[j, side], device_id=to, device_id_type=MESH,
        )

    def ocean_sends():
        copies = []
        for g in range(3):
            copies.append(across_edge(g, 0, dev_id((g * TILES + tile + 95) % 96), 0))
            copies.append(across_edge(g, 1, dev_id((g * TILES + tile + 1) % 96), 0))
            copies.append(across(g, ps.at[g], (g, tile), 0))
        return copies

    def air_sends():
        return [
            across_edge(0, 0, (3, t_prev), grp),
            across_edge(0, 1, (3, t_next), grp),
            across(0, ps.at[0], (3, tile), grp),
        ]

    @pl.when(ocean)
    def _():
        for d in ocean_sends():
            d.start()
        for j in range(3):
            across(j, ps.at[0], (0, tile), j).wait_recv()
            for side in range(2):
                across_edge(j, side, (0, tile), j).wait_recv()

    @pl.when(jnp.logical_not(ocean))
    def _():
        for d in air_sends():
            d.start()
        for j in range(1, 3):
            xr[j] = jnp.zeros(xr.shape[1:], F32)
            xe[j] = jnp.zeros(xe.shape[1:], F32)
        across(0, ps.at[0], (3, tile), 0).wait_recv()
        for side in range(2):
            across_edge(0, side, (3, tile), 0).wait_recv()

    forc, f_up, f_dn = [], [], []
    e_up = (xe[0, 1] + xe[1, 1] + xe[2, 1]) * GAIN
    e_dn = (xe[0, 0] + xe[1, 0] + xe[2, 0]) * GAIN
    for c in range(CB):
        tot = None
        for f in range(F):
            r = xr[0, c, f] + xr[1, c, f] + xr[2, c, f]
            rec_h[f, :, c * 128:(c + 1) * 128] = r
            tot = r if tot is None else tot + r
        forc.append(GAIN * wets[c] * tot)
        f_up.append(e_up[c:c + 1] * wet_up[c])
        f_dn.append(e_dn[c:c + 1] * wet_dn[c])
    for d in edge_u:
        d.wait_recv()

    def level(l):
        x = [uu[c, l] + gg[c, l] * forc[c] for c in range(CB)]
        up = [
            ru[1, 0, c, pl.ds(l, 1), :] + ru[1, 1, c, pl.ds(l, 1), :] * f_up[c] for c in range(CB)
        ]
        dn = [
            ru[0, 0, c, pl.ds(l, 1), :] + ru[0, 1, c, pl.ds(l, 1), :] * f_dn[c] for c in range(CB)
        ]
        return spread(x, up, dn)

    def second(i, carry):
        r_t, r_b = carry
        l_t, l_b = i, LEV - 1 - i
        h_t, h_b = level(l_t), level(l_b)
        n_t, n_b = [], []
        for c in range(CB):
            r = h_t[c] + r_t[c]
            s = h_b[c] + r_b[c]
            ru_fwd[c, l_t] = r
            ru_fwd[c, l_b] = s
            n_t.append(ww[c, l_t] * r)
            n_b.append(ww[c, l_b] * s)
        return n_t, n_b

    r_t, _ = lax.fori_loop(0, HALF, second, (forc, zeros), unroll=4)
    x_t, x_b = [], []
    for c in range(CB):
        x32 = (ru_fwd[c, HALF] + r_t[c]) * mid[c]
        x_t.append(x32)
        x_b.append(inv[c, HALF - 1] * ru_fwd[c, HALF - 1] + ww[c, HALF - 1] * x32)

    def back2(i, carry):
        x_t, x_b = carry
        l_t, l_b = HALF - 1 - i, HALF + i
        n_t, n_b = [], []
        for c in range(CB):
            x0 = inv[c, l_t] * ru_fwd[c, l_t] + ww[c, l_t] * x_t[c]
            x1 = inv[c, l_b] * ru_fwd[c, l_b] + ww[c, l_b] * x_b[c]
            out_h[l_t, :, c * 128:(c + 1) * 128] = x0
            out_h[l_b, :, c * 128:(c + 1) * 128] = x1
            n_t.append(x0)
            n_b.append(x1)
        return n_t, n_b

    lax.fori_loop(0, HALF, back2, (x_t, x_b), unroll=8)
    for d in edge + edge_u:
        d.wait_send()

    @pl.loop(1, TILES)
    def _(d):
        a2a(d).wait_send()

    @pl.when(ocean)
    def _():
        for d in ocean_sends():
            d.wait_send()

    @pl.when(jnp.logical_not(ocean))
    def _():
        for d in air_sends():
            d.wait_send()


def local(*args):
    vm = pltpu.VMEM
    dma = pltpu.SemaphoreType.DMA
    col = (CB, LEV, 8, 128)
    scratch = [
        vm((32, K, 128, 128), BF16), vm((8, 512), F32), vm(col, F32), vm((CB, LEV - 1, 8, 128), F32),
        vm((8, 512), F32), vm((8, 512), jnp.int32), vm((F, 8, 512), F32), vm((F, 8, 512), F32),
        vm((K, 32), jnp.int32), vm((K, 32), jnp.int32), vm((K, 32), jnp.int32),
        vm((128, 128), F32), vm((512, 128), F32),
        vm((TILES * MSG, 128), F32), vm((TILES * MSG, 128), F32),
        vm((3, CB, F, 8, 128), F32), vm((3, CB, F, 8, 128), F32),
        vm((3, 2, 8, 128), F32), vm((3, 2, 8, 128), F32),
        vm((2, CB, LEV + 8, 128), F32), vm((2, CB, LEV + 8, 128), F32),
        vm((2, 2, CB, LEV, 128), F32), vm((2, 2, CB, LEV, 128), F32),
        vm((5, CB, 8, 128), F32), vm((CB, 8, 128), F32),
        vm(col, F32), vm(col, F32), vm((CB, 8, 128), F32),
        vm((CB, HALF, 8, 128), F32), vm(col, F32), vm(col, F32), vm(col, F32),
        dma((16,)), dma((WCH,)), dma((TILES,)), dma((TILES,)), dma((2, 2)), dma((2, 2)),
        dma((3,)), dma((3,)), dma((3, 2)), dma((3, 2)),
    ]
    hbm = pl.BlockSpec(memory_space=pltpu.HBM)
    out = pl.BlockSpec(memory_space=pltpu.VMEM)
    return pl.pallas_call(
        kernel,
        out_shape=(
            vm((LEV, 8, 512), F32), vm((F, 8, 512), F32),
        ),
        in_specs=[hbm] * 10,
        out_specs=(out, out),
        scratch_shapes=scratch,
        compiler_params=pltpu.CompilerParams(
            collective_id=0, has_side_effects=True, vmem_limit_bytes=50 * 1024 * 1024
        ),
        name="window",
    )(*(pltpu.with_memory_space_constraint(a, pltpu.HBM) for a in (*args[:7], *(a.T for a in args[7:]))))


def solution(mesh):
    both = ("grp", "tile")
    in_specs = (
        P(None, both, None), P(None, both, None), P(both, None), P("tile", None),
        P(None, both, None), P(None, both, None), P(both, None, None, None),
        P(both, None), P(both, None), P(both, None),
    )
    out_specs = (P(None, both, None), P(None, both, None))
    return jax.shard_map(local, mesh=mesh, in_specs=in_specs, out_specs=out_specs, check_vma=False)
```

```python
import functools

import jax
import jax.numpy as jnp
from jax import lax
from jax.experimental import pallas as pl
from jax.experimental.pallas import tpu as pltpu
from jax.sharding import PartitionSpec as P

MESH = pl.DeviceIdType.MESH
F32 = jnp.float32
BF16 = jnp.bfloat16
F = 4
K = 4
LEV = 64
HALF = LEV // 2
TILES = 32
SLOTS = 8
MSG = 40
SENT = 33
CB = 4
WCH = 8
HR = 3 * LEV + 8
GAIN = 0.25


def iota(shape, dim):
    return lax.broadcasted_iota(jnp.int32, shape, dim)


def one_hot(mask):
    return jnp.where(mask, 1.0, 0.0).astype(BF16)


def split(x):
    hi = x.astype(BF16)
    return hi, (x - hi.astype(F32)).astype(BF16)


def kernel(
    state_h, vert_h, nu_h, mask_h, coup_h, surf_h, w_h, dt_h, db_h, dg_h,
    out_h, rec_h,
    w_v, s0, st, ve, nu, mask, coup, surf, dt, db, dg,
    xs, terms, slab, got, ps, xr, es, xe,
    se, re, xh, coef, coef_h, wet, inv, ww, mid, rg, ru_fwd, uu, gg,
    lsem, wsem, ssem, rsem, hs, hr, xss, xrs, ess, ers,
):
    grp = lax.axis_index("grp")
    tile = lax.axis_index("tile")
    dev = grp * TILES + tile
    ocean = grp == 3
    n_dev = 4 * TILES

    def dev_id(flat):
        return (flat // TILES, flat % TILES)

    above_dev = dev_id((dev + n_dev - 1) % n_dev)
    below_dev = dev_id((dev + 1) % n_dev)
    t_prev, t_next = (tile + TILES - 1) % TILES, (tile + 1) % TILES

    barrier = pltpu.get_barrier_semaphore()

    def tell(device):
        pl.semaphore_signal(barrier, inc=1, device_id=device, device_id_type=MESH)

    @pl.loop(1, TILES)
    def _(d):
        tell((grp, (tile + d) % TILES))

    tell(above_dev)
    tell(below_dev)

    @pl.when(ocean)
    def _():
        for g in range(3):
            for t in (tile, t_prev, t_next):
                tell((g, t))

    @pl.when(jnp.logical_not(ocean))
    def _():
        for t in (tile, t_prev, t_next):
            tell((3, t))

    def load(src, dst, i):
        return pltpu.make_async_copy(src, dst, lsem.at[i])

    small = [
        load(dt_h, dt, 0), load(db_h, db, 1), load(dg_h, dg, 2),
        load(mask_h, mask, 3), load(coup_h, coup, 4), load(surf_h, surf, 5), load(nu_h, nu, 6),
        load(state_h.at[0], s0, 15),
    ]
    st_load = [load(state_h.at[:, :, c * 128:(c + 1) * 128], st.at[c], 7 + c) for c in range(CB)]
    ve_load = [
        load(vert_h.at[:, :, c * 128:(c + 1) * 128], ve.at[c], 11 + c) for c in range(CB)
    ]
    per = 32 // WCH
    w_load = [
        pltpu.make_async_copy(w_h.at[pl.ds(i * per, per)], w_v.at[pl.ds(i * per, per)], wsem.at[i])
        for i in range(WCH)
    ]
    for d in small + w_load + st_load + ve_load:
        d.start()

    for d in small:
        d.wait()

    lane = iota((1, 128), 1)
    k_of = lane % 4
    b_of = 2 * ((lane % 64) // 4) + lane // 64
    group_label = jnp.where(ocean, 32, 0)
    both = jnp.concatenate(
        [((dt[...] + TILES - tile) % TILES).astype(F32),
         (db[...] + dg[...] * group_label + 1).astype(F32)], axis=0
    ).astype(BF16)
    wide = jnp.dot(both, one_hot(iota((32, 128), 0) == b_of), preferred_element_type=F32)
    of_k = iota((K, 128), 0) == k_of
    d_row = jnp.sum(jnp.where(of_k, wide[:K], 0.0), axis=0, keepdims=True)
    label = jnp.sum(jnp.where(of_k, wide[K:], 0.0), axis=0, keepdims=True)
    drel = d_row.astype(jnp.int32)
    i0, i1 = iota((128, 128), 0), iota((128, 128), 1)
    d_col = jnp.sum(jnp.where(i0 == i1, d_row, 0.0), axis=1, keepdims=True)
    pos = jnp.sum(jnp.where((d_col == d_row) & (i0 < i1), 1.0, 0.0), axis=0, keepdims=True)
    slot = drel * SLOTS + pos.astype(jnp.int32)
    tag_a = jnp.where(iota((TILES, 128), 0) == drel, label, 0.0).astype(BF16)
    tag_b = one_hot(i0 == slot % 128)
    tags = lax.dot_general(tag_a, tag_b, (((1,), (1,)), ((), ())), preferred_element_type=F32)
    for j in range(TILES // 8):
        slab[pl.ds(j * 8 * MSG + 32, 8, stride=MSG), :] = tags[j * 8:(j + 1) * 8]

    for c in range(CB):
        cs = slice(c * 128, (c + 1) * 128)
        wet_c = jnp.where(ocean, mask[:, cs].astype(F32), 1.0)
        wet[c] = wet_c
        for f in range(F):
            send = coup[f, :, cs] * (s0[:, cs] - surf[f, :, cs]) * wet_c
            xs[pl.ds(c * 4 + f, 8, stride=16), :] = send

    row8 = iota((8, 128), 0)

    def two_blocks(q):
        x8 = xs[pl.ds(q * 8, 8), :]
        x = jnp.concatenate(
            [jnp.where(row8 < 4, x8, 0.0), jnp.where(row8 < 4, 0.0, x8)], axis=1
        ).astype(BF16)
        for kp in range(2):
            cols = [w_v[pl.ds(2 * q, 2), 2 * kp + j].reshape(256, 128) for j in range(2)]
            t = jnp.dot(x, jnp.concatenate(cols, axis=1), preferred_element_type=F32)
            for j in range(2):
                terms[pl.ds(q * 4 + 2 * kp + j, 8, stride=64), :] = t[:, j * 128:(j + 1) * 128]

    for i in range(WCH):
        w_load[i].wait()
        for q in range(i * 16 // WCH, (i + 1) * 16 // WCH):
            two_blocks(q)

    his, los = [], []
    for f in range(F):
        t = jnp.concatenate([terms[bl * 256 + f * 64:bl * 256 + f * 64 + 64, :] for bl in range(2)], 0)
        hi, lo = split(t)
        his.append(hi)
        los.append(lo)
    hi = jnp.concatenate(his, axis=1)
    lo = jnp.concatenate(los, axis=1)

    def a2a(d):
        return pltpu.make_async_remote_copy(
            src_ref=slab.at[pl.ds(d * MSG, SENT)], dst_ref=got.at[pl.ds(d * MSG, SENT)],
            send_sem=ssem.at[d], recv_sem=rsem.at[d],
            device_id=(grp, (tile + d) % TILES), device_id_type=MESH,
        )

    parts = 4
    rows = TILES * SLOTS // parts
    for p in range(parts):
        ch = one_hot(iota((rows, 128), 0) + p * rows == slot)
        packed = jnp.dot(ch, hi, preferred_element_type=F32) + jnp.dot(
            ch, lo, preferred_element_type=F32
        )
        for j in range(TILES // parts):
            d = p * (TILES // parts) + j
            for f in range(F):
                slab[d * MSG + f * 8:d * MSG + f * 8 + 8, :] = packed[
                    j * 8:(j + 1) * 8, f * 128:(f + 1) * 128
                ]

    for d in st_load + ve_load:
        d.wait()
    for c in range(CB):
        rows = st.at[c].reshape(LEV * 8, 128)
        rows_v = ve.at[c].reshape((LEV - 1) * 8, 128)
        for side in range(2):
            near, far = 7 * side, 1 + 5 * side
            se[side, c, 0:LEV, :] = rows[pl.ds(near, LEV, stride=8), :]
            se[side, c, LEV:2 * LEV, :] = rows[pl.ds(far, LEV, stride=8), :]
            se[side, c, 2 * LEV:3 * LEV - 1, :] = rows_v[pl.ds(near, LEV - 1, stride=8), :]
            se[side, c, 3 * LEV:3 * LEV + 1, :] = wet[c, near:near + 1, :]
            se[side, c, 3 * LEV + 1:3 * LEV + 2, :] = wet[c, far:far + 1, :]
            se[side, c, 3 * LEV + 2:3 * LEV + 3, :] = nu[near:near + 1, c * 128:(c + 1) * 128]

    def halo(side):
        return pltpu.make_async_remote_copy(
            src_ref=se.at[side], dst_ref=re.at[side], send_sem=hs.at[side],
            recv_sem=hr.at[side], device_id=above_dev if side == 0 else below_dev,
            device_id_type=MESH,
        )

    @pl.when(ocean)
    def _():
        pl.semaphore_wait(barrier, 31 + 2 + 9)

    @pl.when(jnp.logical_not(ocean))
    def _():
        pl.semaphore_wait(barrier, 31 + 2 + 3)

    @pl.loop(1, TILES)
    def _(d):
        a2a(d).start()

    edge = [halo(side) for side in range(2)]
    to_above, to_below = (dev != 0) & (dev != 96), (dev != 127) & (dev != 95)
    from_above, from_below = (dev != 0) & (dev != 96), (dev != 127) & (dev != 95)

    @pl.when(to_above)
    def _():
        edge[0].start()

    @pl.when(to_below)
    def _():
        edge[1].start()

    inv[0, 0] = jnp.ones((8, 128), F32)
    inv[0, 1] = jnp.zeros((8, 128), F32)
    one, zero = inv[0, 0], inv[0, 1]
    wets = [wet[c] for c in range(CB)]

    def factor(i, carry):
        e_t, e_b, _, r_g = carry
        n_t, n_b, n_g = [], [], []
        for c in range(CB):
            a_t = ve[c, i] * wets[c]
            a_b = ve[c, LEV - 2 - i] * wets[c]
            i_t = 1.0 / (e_t[c] + a_t)
            i_b = 1.0 / (e_b[c] + a_b)
            w_t, w_b = a_t * i_t, a_b * i_b
            inv[c, i] = i_t
            inv[c, LEV - 1 - i] = i_b
            ww[c, i] = w_t
            ww[c, LEV - 1 - i] = w_b
            rg[c, i] = r_g[c]
            n_t.append(1.0 + w_t * e_t[c])
            n_b.append(1.0 + w_b * e_b[c])
            n_g.append(w_t * r_g[c])
        return n_t, n_b, e_b, n_g

    ones = [one] * CB
    zeros = [zero] * CB
    e_t, _, e_b, r_g = lax.fori_loop(0, HALF, factor, (ones, ones, ones, ones), unroll=4)
    mids = [1.0 / (e_t[c] + e_b[c] - 1.0) for c in range(CB)]
    for c in range(CB):
        mid[c] = mids[c]

    y_t, y_b = [], []
    for c in range(CB):
        y_t.append(r_g[c] * mids[c])
        y_b.append(inv[c, HALF - 1] * rg[c, HALF - 1] + ww[c, HALF - 1] * y_t[c])

    def back_g(i, carry):
        y_t, y_b = carry
        l_t, l_b = HALF - 1 - i, HALF + i
        n_t, n_b = [], []
        for c in range(CB):
            y0 = inv[c, l_t] * rg[c, l_t] + ww[c, l_t] * y_t[c]
            y1 = ww[c, l_b] * y_b[c]
            gg[c, l_t] = y0
            gg[c, l_b] = y1
            n_t.append(y0)
            n_b.append(y1)
        return n_t, n_b

    lax.fori_loop(0, HALF, back_g, (y_t, y_b), unroll=4)

    got[0:MSG, :] = slab[0:MSG, :]

    @pl.loop(1, TILES)
    def _(d):
        a2a(d).wait_recv()

    halves = []
    for h in range(2):
        t = got[pl.ds(h * 16 * MSG + 32, 8, stride=MSG), :] + got[
            pl.ds((h * 16 + 8) * MSG + 32, 8, stride=MSG), :
        ]
        halves.append(jnp.sum(t, axis=0, keepdims=True))
    tag_row = jnp.concatenate(halves, axis=1)
    m = iota((96, 256), 0)
    want = (m // 32) * 32 + (m % 8) * 4 + (m % 32) // 8 + 1
    ch2 = one_hot(want.astype(F32) == tag_row)
    for f in range(F):
        items = jnp.concatenate(
            [got[d * MSG + f * 8:d * MSG + f * 8 + 8, :] for d in range(TILES)], axis=0
        )
        hi, lo = split(items)
        part = jnp.dot(ch2, hi, preferred_element_type=F32) + jnp.dot(
            ch2, lo, preferred_element_type=F32
        )
        for g in range(3):
            for c in range(CB):
                ps[g, c, f] = part[g * 32 + c * 8:g * 32 + c * 8 + 8]
    for g in range(3):
        for c in range(CB):
            tot = ps[g, c, 0] + ps[g, c, 1] + ps[g, c, 2] + ps[g, c, 3]
            es[g, 0, c:c + 1, :] = tot[0:1]
            es[g, 1, c:c + 1, :] = tot[7:8]

    def across(g, src, to, j):
        return pltpu.make_async_remote_copy(
            src_ref=src, dst_ref=xr.at[j], send_sem=xss.at[g], recv_sem=xrs.at[j],
            device_id=to, device_id_type=MESH,
        )

    def across_edge(g, side, to, j):
        return pltpu.make_async_remote_copy(
            src_ref=es.at[g, side], dst_ref=xe.at[j, side], send_sem=ess.at[g, side],
            recv_sem=ers.at[j, side], device_id=to, device_id_type=MESH,
        )

    def ocean_sends():
        copies = []
        for g in range(3):
            copies.append(across_edge(g, 0, dev_id((g * TILES + tile + 95) % 96), 0))
            copies.append(across_edge(g, 1, dev_id((g * TILES + tile + 1) % 96), 0))
            copies.append(across(g, ps.at[g], (g, tile), 0))
        return copies

    def air_sends():
        return [
            across_edge(0, 0, (3, t_prev), grp),
            across_edge(0, 1, (3, t_next), grp),
            across(0, ps.at[0], (3, tile), grp),
        ]

    @pl.when(ocean)
    def _():
        for d in ocean_sends():
            d.start()

    @pl.when(jnp.logical_not(ocean))
    def _():
        for d in air_sends():
            d.start()
        for j in range(1, 3):
            xr[j] = jnp.zeros(xr.shape[1:], F32)
            xe[j] = jnp.zeros(xe.shape[1:], F32)

    @pl.when(from_below)
    def _():
        edge[0].wait_recv()

    @pl.when(from_above)
    def _():
        edge[1].wait_recv()

    lane8 = iota((8, 128), 1)
    keep_above = jnp.where((dev != 0) & (dev != 96), 1.0, 0.0)
    keep_below = jnp.where((dev != 127) & (dev != 95), 1.0, 0.0)

    def neighbours(x, up, dn):
        ls = [pltpu.roll(x[c], 1, 1) for c in range(CB)]
        rs = [pltpu.roll(x[c], 127, 1) for c in range(CB)]
        out = []
        for c in range(CB):
            left = ls[c] if c == 0 else jnp.where(lane8 == 0, ls[c - 1], ls[c])
            right = rs[c] if c == CB - 1 else jnp.where(lane8 == 127, rs[c + 1], rs[c])
            above = jnp.where(row8 == 0, up[c], pltpu.roll(x[c], 1, 0))
            below = jnp.where(row8 == 7, dn[c], pltpu.roll(x[c], 7, 0))
            out.append((left, right, above, below))
        return out

    wet_up = [re[1, c, 3 * LEV:3 * LEV + 1, :] for c in range(CB)]
    wet_dn = [re[0, c, 3 * LEV:3 * LEV + 1, :] for c in range(CB)]
    around = neighbours(
        wets, [w * keep_above for w in wet_up], [w * keep_below for w in wet_dn]
    )
    for c in range(CB):
        left, right, above, below = around[c]
        if c == 0:
            left = jnp.where(lane8 == 0, 0.0, left)
        if c == CB - 1:
            right = jnp.where(lane8 == 127, 0.0, right)
        scale = nu[:, c * 128:(c + 1) * 128] * wets[c]
        cs = [scale * v for v in (left, right, above, below)]
        for j in range(4):
            coef[j, c] = cs[j]
        coef[4, c] = 1.0 - (cs[0] + cs[1] + cs[2] + cs[3])

    def spread(x, up, dn):
        out = []
        for c, near in enumerate(neighbours(x, up, dn)):
            total = coef[4, c] * x[c]
            for j in range(4):
                total = total + coef[j, c] * near[j]
            out.append(total)
        return out

    re_rows = re.reshape(2 * CB * HR, 128)
    se_rows = se.reshape(2 * CB * HR, 128)

    def theirs(row):
        return re_rows[pl.ds(row, 8, stride=HR), :]

    def mine(row):
        return pltpu.roll(se_rows[pl.ds(row, 8, stride=HR), :], 4, 0)

    def sideways(x):
        left, right = pltpu.roll(x, 1, 1), pltpu.roll(x, 127, 1)
        left = jnp.where(lane8 == 0, pltpu.roll(left, 1, 0), left)
        right = jnp.where(lane8 == 127, pltpu.roll(right, 7, 0), right)
        return left, right

    wet_h = theirs(3 * LEV)
    left, right = sideways(wet_h)
    left = jnp.where((lane8 == 0) & (row8 % 4 == 0), 0.0, left)
    right = jnp.where((lane8 == 127) & (row8 % 4 == 3), 0.0, right)
    scale = theirs(3 * LEV + 2) * wet_h
    ch = [scale * left, scale * right, scale * theirs(3 * LEV + 1), scale * mine(3 * LEV)]
    ch.append(1.0 - (ch[0] + ch[1] + ch[2] + ch[3]))
    for j in range(5):
        coef_h[j] = ch[j]

    def spread_h(l):
        x = theirs(l)
        left, right = sideways(x)
        return (
            coef_h[4] * x + coef_h[0] * left + coef_h[1] * right
            + coef_h[2] * theirs(LEV + l) + coef_h[3] * mine(l)
        )

    def halo_rows(side, l):
        return [re[side, c, pl.ds(l, 1), :] for c in range(CB)]

    def first(i, carry):
        r_t, r_b, e_t, e_b, _, r_g = carry
        l_t, l_b = i, LEV - 1 - i
        a_t = theirs(2 * LEV + i) * wet_h
        a_b = theirs(3 * LEV - 2 - i) * wet_h
        i_t = 1.0 / (e_t + a_t)
        i_b = 1.0 / (e_b + a_b)
        w_t, w_b = a_t * i_t, a_b * i_b
        inv[CB, l_t] = i_t
        inv[CB, l_b] = i_b
        ww[CB, l_t] = w_t
        ww[CB, l_b] = w_b
        rg[CB, l_t] = r_g
        h_t = spread([st[c, l_t] for c in range(CB)], halo_rows(1, l_t), halo_rows(0, l_t))
        h_b = spread([st[c, l_b] for c in range(CB)], halo_rows(1, l_b), halo_rows(0, l_b))
        h_t.append(spread_h(l_t))
        h_b.append(spread_h(l_b))
        n_t, n_b = [], []
        for c in range(CB + 1):
            r = h_t[c] + r_t[c]
            s = h_b[c] + r_b[c]
            ru_fwd[c, l_t] = r
            ru_fwd[c, l_b] = s
            n_t.append((ww[c, l_t] if c < CB else w_t) * r)
            n_b.append((ww[c, l_b] if c < CB else w_b) * s)
        return n_t, n_b, 1.0 + w_t * e_t, 1.0 + w_b * e_b, e_b, w_t * r_g

    r_t, _, e_t, _, e_b, r_g = lax.fori_loop(
        0, HALF, first, (zeros + [zero], zeros + [zero], one, one, one, one), unroll=4
    )
    mid_h = 1.0 / (e_t + e_b - 1.0)
    x_b, x_t = [], []
    for c in range(CB + 1):
        x_t.append((ru_fwd[c, HALF] + r_t[c]) * (mids[c] if c < CB else mid_h))
        x_b.append(inv[c, HALF - 1] * ru_fwd[c, HALF - 1] + ww[c, HALF - 1] * x_t[c])
    y_t = r_g * mid_h
    y_b = inv[CB, HALF - 1] * rg[CB, HALF - 1] + ww[CB, HALF - 1] * y_t

    def back(i, carry):
        x_t, x_b, y_t, y_b = carry
        l_t, l_b = HALF - 1 - i, HALF + i
        n_t, n_b = [], []
        for c in range(CB + 1):
            w_t, w_b, i_t, i_b = ww[c, l_t], ww[c, l_b], inv[c, l_t], inv[c, l_b]
            x0 = i_t * ru_fwd[c, l_t] + w_t * x_t[c]
            x1 = i_b * ru_fwd[c, l_b] + w_b * x_b[c]
            uu[c, l_t] = x0
            uu[c, l_b] = x1
            n_t.append(x0)
            n_b.append(x1)
        y0 = i_t * rg[CB, l_t] + w_t * y_t
        y1 = w_b * y_b
        gg[CB, l_t] = y0
        gg[CB, l_b] = y1
        return n_t, n_b, y0, y1

    lax.fori_loop(0, HALF, back, (x_t, x_b, y_t, y_b), unroll=4)

    @pl.when(ocean)
    def _():
        for j in range(3):
            across(j, ps.at[0], (0, tile), j).wait_recv()
            for side in range(2):
                across_edge(j, side, (0, tile), j).wait_recv()

    @pl.when(jnp.logical_not(ocean))
    def _():
        across(0, ps.at[0], (3, tile), 0).wait_recv()
        for side in range(2):
            across_edge(0, side, (3, tile), 0).wait_recv()

    forc = []
    e_up = (xe[0, 1] + xe[1, 1] + xe[2, 1]) * GAIN
    e_dn = (xe[0, 0] + xe[1, 0] + xe[2, 0]) * GAIN
    for c in range(CB):
        tot = None
        for f in range(F):
            r = xr[0, c, f] + xr[1, c, f] + xr[2, c, f]
            rec_h[f, :, c * 128:(c + 1) * 128] = r
            tot = r if tot is None else tot + r
        forc.append(GAIN * wets[c] * tot)
    f_h = jnp.where(row8 < 4, e_dn, pltpu.roll(e_up, 4, 0)) * wet_h
    for l in range(LEV):
        xh[l] = uu[CB, l] + gg[CB, l] * f_h


    def level(l):
        x = [uu[c, l] + gg[c, l] * forc[c] for c in range(CB)]
        up = [xh[l, 4 + c:5 + c, :] for c in range(CB)]
        dn = [xh[l, c:c + 1, :] for c in range(CB)]
        return spread(x, up, dn)

    def second(i, carry):
        r_t, r_b = carry
        l_t, l_b = i, LEV - 1 - i
        h_t, h_b = level(l_t), level(l_b)
        n_t, n_b = [], []
        for c in range(CB):
            r = h_t[c] + r_t[c]
            s = h_b[c] + r_b[c]
            ru_fwd[c, l_t] = r
            ru_fwd[c, l_b] = s
            n_t.append(ww[c, l_t] * r)
            n_b.append(ww[c, l_b] * s)
        return n_t, n_b

    r_t, _ = lax.fori_loop(0, HALF, second, (forc, zeros), unroll=4)
    x_t, x_b = [], []
    for c in range(CB):
        x32 = (ru_fwd[c, HALF] + r_t[c]) * mid[c]
        x_t.append(x32)
        x_b.append(inv[c, HALF - 1] * ru_fwd[c, HALF - 1] + ww[c, HALF - 1] * x32)

    def back2(i, carry):
        x_t, x_b = carry
        l_t, l_b = HALF - 1 - i, HALF + i
        n_t, n_b = [], []
        for c in range(CB):
            x0 = inv[c, l_t] * ru_fwd[c, l_t] + ww[c, l_t] * x_t[c]
            x1 = inv[c, l_b] * ru_fwd[c, l_b] + ww[c, l_b] * x_b[c]
            out_h[l_t, :, c * 128:(c + 1) * 128] = x0
            out_h[l_b, :, c * 128:(c + 1) * 128] = x1
            n_t.append(x0)
            n_b.append(x1)
        return n_t, n_b

    lax.fori_loop(0, HALF, back2, (x_t, x_b), unroll=8)
    @pl.when(to_above)
    def _():
        edge[0].wait_send()

    @pl.when(to_below)
    def _():
        edge[1].wait_send()


    @pl.loop(1, TILES)
    def _(d):
        a2a(d).wait_send()

    @pl.when(ocean)
    def _():
        for d in ocean_sends():
            d.wait_send()

    @pl.when(jnp.logical_not(ocean))
    def _():
        for d in air_sends():
            d.wait_send()


def flush(state_v, received_v, state_h, received_h, sem):
    copies = [
        pltpu.make_async_copy(state_v, state_h, sem.at[0]),
        pltpu.make_async_copy(received_v, received_h, sem.at[1]),
    ]
    for d in copies:
        d.start()
    for d in copies:
        d.wait()


def local(*args):
    vm = pltpu.VMEM
    dma = pltpu.SemaphoreType.DMA
    col = (CB, LEV, 8, 128)
    five = (CB + 1, LEV, 8, 128)
    scratch = [
        vm((32, K, 128, 128), BF16), vm((8, 512), F32), vm(col, F32), vm((CB, LEV - 1, 8, 128), F32),
        vm((8, 512), F32), vm((8, 512), jnp.int32), vm((F, 8, 512), F32), vm((F, 8, 512), F32),
        vm((K, 32), jnp.int32), vm((K, 32), jnp.int32), vm((K, 32), jnp.int32),
        vm((128, 128), F32), vm((512, 128), F32),
        vm((TILES * MSG, 128), F32), vm((TILES * MSG, 128), F32),
        vm((3, CB, F, 8, 128), F32), vm((3, CB, F, 8, 128), F32),
        vm((3, 2, 8, 128), F32), vm((3, 2, 8, 128), F32),
        vm((2, CB, HR, 128), F32), vm((2, CB, HR, 128), F32), vm((LEV, 8, 128), F32),
        vm((5, CB, 8, 128), F32), vm((5, 8, 128), F32), vm((CB, 8, 128), F32),
        vm(five, F32), vm(five, F32), vm((CB, 8, 128), F32),
        vm((CB + 1, HALF, 8, 128), F32), vm(five, F32), vm(five, F32), vm(five, F32),
        dma((16,)), dma((WCH,)), dma((TILES,)), dma((TILES,)), dma((2,)), dma((2,)),
        dma((3,)), dma((3,)), dma((3, 2)), dma((3, 2)),
    ]
    hbm = pl.BlockSpec(memory_space=pltpu.HBM)
    out = pl.BlockSpec(memory_space=pltpu.VMEM)
    outs = pl.pallas_call(
        kernel,
        out_shape=(
            vm((LEV, 8, 512), F32), vm((F, 8, 512), F32),
        ),
        in_specs=[hbm] * 10,
        out_specs=(out, out),
        scratch_shapes=scratch,
        compiler_params=pltpu.CompilerParams(
            collective_id=0, has_side_effects=True, vmem_limit_bytes=50 * 1024 * 1024
        ),
        name="window",
    )(*(pltpu.with_memory_space_constraint(a, pltpu.HBM) for a in (*args[:7], *(a.T for a in args[7:]))))
    return pl.pallas_call(
        flush,
        out_shape=(
            jax.ShapeDtypeStruct((LEV, 8, 512), F32), jax.ShapeDtypeStruct((F, 8, 512), F32),
        ),
        in_specs=[pl.BlockSpec(memory_space=pltpu.VMEM)] * 2,
        out_specs=(hbm, hbm),
        scratch_shapes=[dma((2,))],
        name="flush",
    )(*(pltpu.with_memory_space_constraint(a, pltpu.VMEM) for a in outs))


def solution(mesh):
    both = ("grp", "tile")
    in_specs = (
        P(None, both, None), P(None, both, None), P(both, None), P("tile", None),
        P(None, both, None), P(None, both, None), P(both, None, None, None),
        P(both, None), P(both, None), P(both, None),
    )
    out_specs = (P(None, both, None), P(None, both, None))
    return jax.shard_map(local, mesh=mesh, in_specs=in_specs, out_specs=out_specs, check_vma=False)
```

```python
import functools

import jax
import jax.numpy as jnp
from jax import lax
from jax.experimental import pallas as pl
from jax.experimental.pallas import tpu as pltpu
from jax.sharding import PartitionSpec as P

MESH = pl.DeviceIdType.MESH
F32 = jnp.float32
BF16 = jnp.bfloat16
F = 4
K = 4
LEV = 64
HALF = LEV // 2
TILES = 32
SLOTS = 8
MSG = 40
SENT = 33
CB = 4
WCH = 8
HR = 3 * LEV + 8
GAIN = 0.25
OUT = 4


def iota(shape, dim):
    return lax.broadcasted_iota(jnp.int32, shape, dim)


def one_hot(mask):
    return jnp.where(mask, 1.0, 0.0).astype(BF16)


def split(x):
    hi = x.astype(BF16)
    return hi, (x - hi.astype(F32)).astype(BF16)


def kernel(
    state_h, vert_h, nu_h, mask_h, coup_h, surf_h, w_h, dt_h, db_h, dg_h,
    ru_fwd, inv, ww, ends, rec_h,
    w_v, s0, st, ve, nu, mask, coup, surf, dt, db, dg,
    xs, terms, slab, got, ps, xr, es, xe,
    se, re, xh, coef, coef_h, wet, mid, rg, uu, gg,
    lsem, wsem, ssem, rsem, hs, hr, xss, xrs, ess, ers,
):
    grp = lax.axis_index("grp")
    tile = lax.axis_index("tile")
    dev = grp * TILES + tile
    ocean = grp == 3
    n_dev = 4 * TILES

    def dev_id(flat):
        return (flat // TILES, flat % TILES)

    above_dev = dev_id((dev + n_dev - 1) % n_dev)
    below_dev = dev_id((dev + 1) % n_dev)
    t_prev, t_next = (tile + TILES - 1) % TILES, (tile + 1) % TILES

    barrier = pltpu.get_barrier_semaphore()

    def tell(device):
        pl.semaphore_signal(barrier, inc=1, device_id=device, device_id_type=MESH)

    @pl.loop(1, TILES)
    def _(d):
        tell((grp, (tile + d) % TILES))

    tell(above_dev)
    tell(below_dev)

    @pl.when(ocean)
    def _():
        for g in range(3):
            for t in (tile, t_prev, t_next):
                tell((g, t))

    @pl.when(jnp.logical_not(ocean))
    def _():
        for t in (tile, t_prev, t_next):
            tell((3, t))

    def load(src, dst, i):
        return pltpu.make_async_copy(src, dst, lsem.at[i])

    small = [
        load(dt_h, dt, 0), load(db_h, db, 1), load(dg_h, dg, 2),
        load(mask_h, mask, 3), load(coup_h, coup, 4), load(surf_h, surf, 5), load(nu_h, nu, 6),
        load(state_h.at[0], s0, 15),
    ]
    st_load = [load(state_h.at[:, :, c * 128:(c + 1) * 128], st.at[c], 7 + c) for c in range(CB)]
    ve_load = [
        load(vert_h.at[:, :, c * 128:(c + 1) * 128], ve.at[c], 11 + c) for c in range(CB)
    ]
    per = 32 // WCH
    w_load = [
        pltpu.make_async_copy(w_h.at[pl.ds(i * per, per)], w_v.at[pl.ds(i * per, per)], wsem.at[i])
        for i in range(WCH)
    ]
    for d in small + w_load + st_load + ve_load:
        d.start()

    for d in small:
        d.wait()

    lane = iota((1, 128), 1)
    k_of = lane % 4
    b_of = 2 * ((lane % 64) // 4) + lane // 64
    group_label = jnp.where(ocean, 32, 0)
    both = jnp.concatenate(
        [((dt[...] + TILES - tile) % TILES).astype(F32),
         (db[...] + dg[...] * group_label + 1).astype(F32)], axis=0
    ).astype(BF16)
    wide = jnp.dot(both, one_hot(iota((32, 128), 0) == b_of), preferred_element_type=F32)
    of_k = iota((K, 128), 0) == k_of
    d_row = jnp.sum(jnp.where(of_k, wide[:K], 0.0), axis=0, keepdims=True)
    label = jnp.sum(jnp.where(of_k, wide[K:], 0.0), axis=0, keepdims=True)
    drel = d_row.astype(jnp.int32)
    i0, i1 = iota((128, 128), 0), iota((128, 128), 1)
    d_col = jnp.sum(jnp.where(i0 == i1, d_row, 0.0), axis=1, keepdims=True)
    pos = jnp.sum(jnp.where((d_col == d_row) & (i0 < i1), 1.0, 0.0), axis=0, keepdims=True)
    slot = drel * SLOTS + pos.astype(jnp.int32)
    tag_a = jnp.where(iota((TILES, 128), 0) == drel, label, 0.0).astype(BF16)
    tag_b = one_hot(i0 == slot % 128)
    tags = lax.dot_general(tag_a, tag_b, (((1,), (1,)), ((), ())), preferred_element_type=F32)
    for j in range(TILES // 8):
        slab[pl.ds(j * 8 * MSG + 32, 8, stride=MSG), :] = tags[j * 8:(j + 1) * 8]

    for c in range(CB):
        cs = slice(c * 128, (c + 1) * 128)
        wet_c = jnp.where(ocean, mask[:, cs].astype(F32), 1.0)
        wet[c] = wet_c
        for f in range(F):
            send = coup[f, :, cs] * (s0[:, cs] - surf[f, :, cs]) * wet_c
            xs[pl.ds(c * 4 + f, 8, stride=16), :] = send

    row8 = iota((8, 128), 0)

    def two_blocks(q):
        x8 = xs[pl.ds(q * 8, 8), :]
        x = jnp.concatenate(
            [jnp.where(row8 < 4, x8, 0.0), jnp.where(row8 < 4, 0.0, x8)], axis=1
        ).astype(BF16)
        for kp in range(2):
            cols = [w_v[pl.ds(2 * q, 2), 2 * kp + j].reshape(256, 128) for j in range(2)]
            t = jnp.dot(x, jnp.concatenate(cols, axis=1), preferred_element_type=F32)
            for j in range(2):
                terms[pl.ds(q * 4 + 2 * kp + j, 8, stride=64), :] = t[:, j * 128:(j + 1) * 128]

    for i in range(WCH):
        w_load[i].wait()
        for q in range(i * 16 // WCH, (i + 1) * 16 // WCH):
            two_blocks(q)

    his, los = [], []
    for f in range(F):
        t = jnp.concatenate([terms[bl * 256 + f * 64:bl * 256 + f * 64 + 64, :] for bl in range(2)], 0)
        hi, lo = split(t)
        his.append(hi)
        los.append(lo)
    hi = jnp.concatenate(his, axis=1)
    lo = jnp.concatenate(los, axis=1)

    def a2a(d):
        return pltpu.make_async_remote_copy(
            src_ref=slab.at[pl.ds(d * MSG, SENT)], dst_ref=got.at[pl.ds(d * MSG, SENT)],
            send_sem=ssem.at[d], recv_sem=rsem.at[d],
            device_id=(grp, (tile + d) % TILES), device_id_type=MESH,
        )

    parts = 4
    rows = TILES * SLOTS // parts
    for p in range(parts):
        ch = one_hot(iota((rows, 128), 0) + p * rows == slot)
        packed = jnp.dot(ch, hi, preferred_element_type=F32) + jnp.dot(
            ch, lo, preferred_element_type=F32
        )
        for j in range(TILES // parts):
            d = p * (TILES // parts) + j
            for f in range(F):
                slab[d * MSG + f * 8:d * MSG + f * 8 + 8, :] = packed[
                    j * 8:(j + 1) * 8, f * 128:(f + 1) * 128
                ]

    for d in st_load + ve_load:
        d.wait()
    for c in range(CB):
        rows = st.at[c].reshape(LEV * 8, 128)
        rows_v = ve.at[c].reshape((LEV - 1) * 8, 128)
        for side in range(2):
            near, far = 7 * side, 1 + 5 * side
            se[side, c, 0:LEV, :] = rows[pl.ds(near, LEV, stride=8), :]
            se[side, c, LEV:2 * LEV, :] = rows[pl.ds(far, LEV, stride=8), :]
            se[side, c, 2 * LEV:3 * LEV - 1, :] = rows_v[pl.ds(near, LEV - 1, stride=8), :]
            se[side, c, 3 * LEV:3 * LEV + 1, :] = wet[c, near:near + 1, :]
            se[side, c, 3 * LEV + 1:3 * LEV + 2, :] = wet[c, far:far + 1, :]
            se[side, c, 3 * LEV + 2:3 * LEV + 3, :] = nu[near:near + 1, c * 128:(c + 1) * 128]

    def halo(side):
        return pltpu.make_async_remote_copy(
            src_ref=se.at[side], dst_ref=re.at[side], send_sem=hs.at[side],
            recv_sem=hr.at[side], device_id=above_dev if side == 0 else below_dev,
            device_id_type=MESH,
        )

    @pl.when(ocean)
    def _():
        pl.semaphore_wait(barrier, 31 + 2 + 9)

    @pl.when(jnp.logical_not(ocean))
    def _():
        pl.semaphore_wait(barrier, 31 + 2 + 3)

    @pl.loop(1, TILES)
    def _(d):
        a2a((d * 13) % TILES).start()

    edge = [halo(side) for side in range(2)]
    to_above, to_below = (dev != 0) & (dev != 96), (dev != 127) & (dev != 95)
    from_above, from_below = (dev != 0) & (dev != 96), (dev != 127) & (dev != 95)

    @pl.when(to_above)
    def _():
        edge[0].start()

    @pl.when(to_below)
    def _():
        edge[1].start()

    inv[0, 0] = jnp.ones((8, 128), F32)
    inv[0, 1] = jnp.zeros((8, 128), F32)
    one, zero = inv[0, 0], inv[0, 1]
    wets = [wet[c] for c in range(CB)]

    def factor(i, carry):
        e_t, e_b, _, r_g = carry
        n_t, n_b, n_g = [], [], []
        for c in range(CB):
            a_t = ve[c, i] * wets[c]
            a_b = ve[c, LEV - 2 - i] * wets[c]
            i_t = 1.0 / (e_t[c] + a_t)
            i_b = 1.0 / (e_b[c] + a_b)
            w_t, w_b = a_t * i_t, a_b * i_b
            inv[c, i] = i_t
            inv[c, LEV - 1 - i] = i_b
            ww[c, i] = w_t
            ww[c, LEV - 1 - i] = w_b
            rg[c, i] = r_g[c]
            n_t.append(1.0 + w_t * e_t[c])
            n_b.append(1.0 + w_b * e_b[c])
            n_g.append(w_t * r_g[c])
        return n_t, n_b, e_b, n_g

    ones = [one] * CB
    zeros = [zero] * CB
    e_t, _, e_b, r_g = lax.fori_loop(0, HALF, factor, (ones, ones, ones, ones), unroll=4)
    mids = [1.0 / (e_t[c] + e_b[c] - 1.0) for c in range(CB)]
    for c in range(CB):
        mid[c] = mids[c]

    y_t, y_b = [], []
    for c in range(CB):
        y_t.append(r_g[c] * mids[c])
        y_b.append(inv[c, HALF - 1] * rg[c, HALF - 1] + ww[c, HALF - 1] * y_t[c])

    def back_g(i, carry):
        y_t, y_b = carry
        l_t, l_b = HALF - 1 - i, HALF + i
        n_t, n_b = [], []
        for c in range(CB):
            y0 = inv[c, l_t] * rg[c, l_t] + ww[c, l_t] * y_t[c]
            y1 = ww[c, l_b] * y_b[c]
            gg[c, l_t] = y0
            gg[c, l_b] = y1
            n_t.append(y0)
            n_b.append(y1)
        return n_t, n_b

    lax.fori_loop(0, HALF, back_g, (y_t, y_b), unroll=4)

    got[0:MSG, :] = slab[0:MSG, :]

    @pl.loop(1, TILES)
    def _(d):
        a2a(d).wait_recv()

    halves = []
    for h in range(2):
        t = got[pl.ds(h * 16 * MSG + 32, 8, stride=MSG), :] + got[
            pl.ds((h * 16 + 8) * MSG + 32, 8, stride=MSG), :
        ]
        halves.append(jnp.sum(t, axis=0, keepdims=True))
    tag_row = jnp.concatenate(halves, axis=1)
    m = iota((96, 256), 0)
    want = (m // 32) * 32 + (m % 8) * 4 + (m % 32) // 8 + 1
    ch2 = one_hot(want.astype(F32) == tag_row)
    for f in range(F):
        items = jnp.concatenate(
            [got[d * MSG + f * 8:d * MSG + f * 8 + 8, :] for d in range(TILES)], axis=0
        )
        hi, lo = split(items)
        part = jnp.dot(ch2, hi, preferred_element_type=F32) + jnp.dot(
            ch2, lo, preferred_element_type=F32
        )
        for g in range(3):
            for c in range(CB):
                ps[g, c, f] = part[g * 32 + c * 8:g * 32 + c * 8 + 8]
    for g in range(3):
        for c in range(CB):
            tot = ps[g, c, 0] + ps[g, c, 1] + ps[g, c, 2] + ps[g, c, 3]
            es[g, 0, c:c + 1, :] = tot[0:1]
            es[g, 1, c:c + 1, :] = tot[7:8]

    def across(g, src, to, j):
        return pltpu.make_async_remote_copy(
            src_ref=src, dst_ref=xr.at[j], send_sem=xss.at[g], recv_sem=xrs.at[j],
            device_id=to, device_id_type=MESH,
        )

    def across_edge(g, side, to, j):
        return pltpu.make_async_remote_copy(
            src_ref=es.at[g, side], dst_ref=xe.at[j, side], send_sem=ess.at[g, side],
            recv_sem=ers.at[j, side], device_id=to, device_id_type=MESH,
        )

    def ocean_sends():
        copies = []
        for g in range(3):
            copies.append(across_edge(g, 0, dev_id((g * TILES + tile + 95) % 96), 0))
            copies.append(across_edge(g, 1, dev_id((g * TILES + tile + 1) % 96), 0))
            copies.append(across(g, ps.at[g], (g, tile), 0))
        return copies

    def air_sends():
        return [
            across_edge(0, 0, (3, t_prev), grp),
            across_edge(0, 1, (3, t_next), grp),
            across(0, ps.at[0], (3, tile), grp),
        ]

    @pl.when(ocean)
    def _():
        for d in ocean_sends():
            d.start()

    @pl.when(jnp.logical_not(ocean))
    def _():
        for d in air_sends():
            d.start()
        for j in range(1, 3):
            xr[j] = jnp.zeros(xr.shape[1:], F32)
            xe[j] = jnp.zeros(xe.shape[1:], F32)

    @pl.when(from_below)
    def _():
        edge[0].wait_recv()

    @pl.when(from_above)
    def _():
        edge[1].wait_recv()

    lane8 = iota((8, 128), 1)
    keep_above = jnp.where((dev != 0) & (dev != 96), 1.0, 0.0)
    keep_below = jnp.where((dev != 127) & (dev != 95), 1.0, 0.0)

    def neighbours(x, up, dn):
        ls = [pltpu.roll(x[c], 1, 1) for c in range(CB)]
        rs = [pltpu.roll(x[c], 127, 1) for c in range(CB)]
        out = []
        for c in range(CB):
            left = ls[c] if c == 0 else jnp.where(lane8 == 0, ls[c - 1], ls[c])
            right = rs[c] if c == CB - 1 else jnp.where(lane8 == 127, rs[c + 1], rs[c])
            above = jnp.where(row8 == 0, up[c], pltpu.roll(x[c], 1, 0))
            below = jnp.where(row8 == 7, dn[c], pltpu.roll(x[c], 7, 0))
            out.append((left, right, above, below))
        return out

    wet_up = [re[1, c, 3 * LEV:3 * LEV + 1, :] for c in range(CB)]
    wet_dn = [re[0, c, 3 * LEV:3 * LEV + 1, :] for c in range(CB)]
    around = neighbours(
        wets, [w * keep_above for w in wet_up], [w * keep_below for w in wet_dn]
    )
    for c in range(CB):
        left, right, above, below = around[c]
        if c == 0:
            left = jnp.where(lane8 == 0, 0.0, left)
        if c == CB - 1:
            right = jnp.where(lane8 == 127, 0.0, right)
        scale = nu[:, c * 128:(c + 1) * 128] * wets[c]
        cs = [scale * v for v in (left, right, above, below)]
        for j in range(4):
            coef[j, c] = cs[j]
        coef[4, c] = 1.0 - (cs[0] + cs[1] + cs[2] + cs[3])

    def spread(x, up, dn):
        out = []
        for c, near in enumerate(neighbours(x, up, dn)):
            total = coef[4, c] * x[c]
            for j in range(4):
                total = total + coef[j, c] * near[j]
            out.append(total)
        return out

    re_rows = re.reshape(2 * CB * HR, 128)
    se_rows = se.reshape(2 * CB * HR, 128)

    def theirs(row):
        return re_rows[pl.ds(row, 8, stride=HR), :]

    def mine(row):
        return pltpu.roll(se_rows[pl.ds(row, 8, stride=HR), :], 4, 0)

    def sideways(x):
        left, right = pltpu.roll(x, 1, 1), pltpu.roll(x, 127, 1)
        left = jnp.where(lane8 == 0, pltpu.roll(left, 1, 0), left)
        right = jnp.where(lane8 == 127, pltpu.roll(right, 7, 0), right)
        return left, right

    wet_h = theirs(3 * LEV)
    left, right = sideways(wet_h)
    left = jnp.where((lane8 == 0) & (row8 % 4 == 0), 0.0, left)
    right = jnp.where((lane8 == 127) & (row8 % 4 == 3), 0.0, right)
    scale = theirs(3 * LEV + 2) * wet_h
    ch = [scale * left, scale * right, scale * theirs(3 * LEV + 1), scale * mine(3 * LEV)]
    ch.append(1.0 - (ch[0] + ch[1] + ch[2] + ch[3]))
    for j in range(5):
        coef_h[j] = ch[j]

    def spread_h(l):
        x = theirs(l)
        left, right = sideways(x)
        return (
            coef_h[4] * x + coef_h[0] * left + coef_h[1] * right
            + coef_h[2] * theirs(LEV + l) + coef_h[3] * mine(l)
        )

    def halo_rows(side, l):
        return [re[side, c, pl.ds(l, 1), :] for c in range(CB)]

    def first(i, carry):
        r_t, r_b, e_t, e_b, _, r_g = carry
        l_t, l_b = i, LEV - 1 - i
        a_t = theirs(2 * LEV + i) * wet_h
        a_b = theirs(3 * LEV - 2 - i) * wet_h
        i_t = 1.0 / (e_t + a_t)
        i_b = 1.0 / (e_b + a_b)
        w_t, w_b = a_t * i_t, a_b * i_b
        inv[CB, l_t] = i_t
        inv[CB, l_b] = i_b
        ww[CB, l_t] = w_t
        ww[CB, l_b] = w_b
        rg[CB, l_t] = r_g
        h_t = spread([st[c, l_t] for c in range(CB)], halo_rows(1, l_t), halo_rows(0, l_t))
        h_b = spread([st[c, l_b] for c in range(CB)], halo_rows(1, l_b), halo_rows(0, l_b))
        h_t.append(spread_h(l_t))
        h_b.append(spread_h(l_b))
        n_t, n_b = [], []
        for c in range(CB + 1):
            r = h_t[c] + r_t[c]
            s = h_b[c] + r_b[c]
            ru_fwd[c, l_t] = r
            ru_fwd[c, l_b] = s
            n_t.append((ww[c, l_t] if c < CB else w_t) * r)
            n_b.append((ww[c, l_b] if c < CB else w_b) * s)
        return n_t, n_b, 1.0 + w_t * e_t, 1.0 + w_b * e_b, e_b, w_t * r_g

    r_t, _, e_t, _, e_b, r_g = lax.fori_loop(
        0, HALF, first, (zeros + [zero], zeros + [zero], one, one, one, one), unroll=4
    )
    mid_h = 1.0 / (e_t + e_b - 1.0)
    x_b, x_t = [], []
    for c in range(CB + 1):
        x_t.append((ru_fwd[c, HALF] + r_t[c]) * (mids[c] if c < CB else mid_h))
        x_b.append(inv[c, HALF - 1] * ru_fwd[c, HALF - 1] + ww[c, HALF - 1] * x_t[c])
    y_t = r_g * mid_h
    y_b = inv[CB, HALF - 1] * rg[CB, HALF - 1] + ww[CB, HALF - 1] * y_t

    def back(i, carry):
        x_t, x_b, y_t, y_b = carry
        l_t, l_b = HALF - 1 - i, HALF + i
        n_t, n_b = [], []
        for c in range(CB + 1):
            w_t, w_b, i_t, i_b = ww[c, l_t], ww[c, l_b], inv[c, l_t], inv[c, l_b]
            x0 = i_t * ru_fwd[c, l_t] + w_t * x_t[c]
            x1 = i_b * ru_fwd[c, l_b] + w_b * x_b[c]
            uu[c, l_t] = x0
            uu[c, l_b] = x1
            n_t.append(x0)
            n_b.append(x1)
        y0 = i_t * rg[CB, l_t] + w_t * y_t
        y1 = w_b * y_b
        gg[CB, l_t] = y0
        gg[CB, l_b] = y1
        return n_t, n_b, y0, y1

    lax.fori_loop(0, HALF, back, (x_t, x_b, y_t, y_b), unroll=4)

    @pl.when(ocean)
    def _():
        for j in range(3):
            across(j, ps.at[0], (0, tile), j).wait_recv()
            for side in range(2):
                across_edge(j, side, (0, tile), j).wait_recv()

    @pl.when(jnp.logical_not(ocean))
    def _():
        across(0, ps.at[0], (3, tile), 0).wait_recv()
        for side in range(2):
            across_edge(0, side, (3, tile), 0).wait_recv()

    forc = []
    e_up = (xe[0, 1] + xe[1, 1] + xe[2, 1]) * GAIN
    e_dn = (xe[0, 0] + xe[1, 0] + xe[2, 0]) * GAIN
    for c in range(CB):
        tot = None
        for f in range(F):
            r = xr[0, c, f] + xr[1, c, f] + xr[2, c, f]
            rec_h[f, :, c * 128:(c + 1) * 128] = r
            tot = r if tot is None else tot + r
        forc.append(GAIN * wets[c] * tot)
    f_h = jnp.where(row8 < 4, e_dn, pltpu.roll(e_up, 4, 0)) * wet_h
    for l in range(LEV):
        xh[l] = uu[CB, l] + gg[CB, l] * f_h


    def level(l):
        x = [uu[c, l] + gg[c, l] * forc[c] for c in range(CB)]
        up = [xh[l, 4 + c:5 + c, :] for c in range(CB)]
        dn = [xh[l, c:c + 1, :] for c in range(CB)]
        return spread(x, up, dn)

    def second(i, carry):
        r_t, r_b = carry
        l_t, l_b = i, LEV - 1 - i
        h_t, h_b = level(l_t), level(l_b)
        n_t, n_b = [], []
        for c in range(CB):
            r = h_t[c] + r_t[c]
            s = h_b[c] + r_b[c]
            ru_fwd[c, l_t] = r
            ru_fwd[c, l_b] = s
            n_t.append(ww[c, l_t] * r)
            n_b.append(ww[c, l_b] * s)
        return n_t, n_b

    r_t, _ = lax.fori_loop(0, HALF, second, (forc, zeros), unroll=8)
    for c in range(CB):
        x32 = (ru_fwd[c, HALF] + r_t[c]) * mid[c]
        ends[0, c] = x32
        ends[1, c] = inv[c, HALF - 1] * ru_fwd[c, HALF - 1] + ww[c, HALF - 1] * x32

    @pl.when(to_above)
    def _():
        edge[0].wait_send()

    @pl.when(to_below)
    def _():
        edge[1].wait_send()


    @pl.loop(1, TILES)
    def _(d):
        a2a(d).wait_send()

    @pl.when(ocean)
    def _():
        for d in ocean_sends():
            d.wait_send()

    @pl.when(jnp.logical_not(ocean))
    def _():
        for d in air_sends():
            d.wait_send()


def finish(fwd, inv, ww, ends, received_v, state_h, received_h, out, sem):
    copies = [pltpu.make_async_copy(received_v, received_h, sem.at[0])]
    copies[0].start()
    step = HALF // OUT

    def back(i, carry):
        x_t, x_b = carry
        l_t, l_b = HALF - 1 - i, HALF + i
        n_t, n_b = [], []
        for c in range(CB):
            cs = slice(c * 128, (c + 1) * 128)
            x0 = inv[c, l_t] * fwd[c, l_t] + ww[c, l_t] * x_t[c]
            x1 = inv[c, l_b] * fwd[c, l_b] + ww[c, l_b] * x_b[c]
            out[l_t, :, cs] = x0
            out[l_b, :, cs] = x1
            n_t.append(x0)
            n_b.append(x1)
        return n_t, n_b

    carry = ([ends[0, c] for c in range(CB)], [ends[1, c] for c in range(CB)])
    for j in range(OUT):
        carry = lax.fori_loop(j * step, (j + 1) * step, back, carry, unroll=step)
        for half, first in enumerate((HALF - (j + 1) * step, HALF + j * step)):
            rows = pl.ds(first, step)
            d = pltpu.make_async_copy(out.at[rows], state_h.at[rows], sem.at[1 + 2 * j + half])
            d.start()
            copies.append(d)
    for d in copies:
        d.wait()


def local(*args):
    vm = pltpu.VMEM
    dma = pltpu.SemaphoreType.DMA
    col = (CB, LEV, 8, 128)
    five = (CB + 1, LEV, 8, 128)
    scratch = [
        vm((32, K, 128, 128), BF16), vm((8, 512), F32), vm(col, F32), vm((CB, LEV - 1, 8, 128), F32),
        vm((8, 512), F32), vm((8, 512), jnp.int32), vm((F, 8, 512), F32), vm((F, 8, 512), F32),
        vm((K, 32), jnp.int32), vm((K, 32), jnp.int32), vm((K, 32), jnp.int32),
        vm((128, 128), F32), vm((512, 128), F32),
        vm((TILES * MSG, 128), F32), vm((TILES * MSG, 128), F32),
        vm((3, CB, F, 8, 128), F32), vm((3, CB, F, 8, 128), F32),
        vm((3, 2, 8, 128), F32), vm((3, 2, 8, 128), F32),
        vm((2, CB, HR, 128), F32), vm((2, CB, HR, 128), F32), vm((LEV, 8, 128), F32),
        vm((5, CB, 8, 128), F32), vm((5, 8, 128), F32), vm((CB, 8, 128), F32),
        vm((CB, 8, 128), F32),
        vm((CB + 1, HALF, 8, 128), F32), vm(five, F32), vm(five, F32),
        dma((16,)), dma((WCH,)), dma((TILES,)), dma((TILES,)), dma((2,)), dma((2,)),
        dma((3,)), dma((3,)), dma((3, 2)), dma((3, 2)),
    ]
    hbm = pl.BlockSpec(memory_space=pltpu.HBM)
    out = pl.BlockSpec(memory_space=pltpu.VMEM)
    outs = pl.pallas_call(
        kernel,
        out_shape=(
            vm(five, F32), vm(five, F32), vm(five, F32), vm((2, CB, 8, 128), F32),
            vm((F, 8, 512), F32),
        ),
        in_specs=[hbm] * 10,
        out_specs=(out,) * 5,
        scratch_shapes=scratch,
        compiler_params=pltpu.CompilerParams(
            collective_id=0, has_side_effects=True, vmem_limit_bytes=50 * 1024 * 1024
        ),
        name="window",
    )(*(pltpu.with_memory_space_constraint(a, pltpu.HBM) for a in (*args[:7], *(a.T for a in args[7:]))))
    return pl.pallas_call(
        finish,
        out_shape=(
            jax.ShapeDtypeStruct((LEV, 8, 512), F32), jax.ShapeDtypeStruct((F, 8, 512), F32),
        ),
        in_specs=[pl.BlockSpec(memory_space=pltpu.VMEM)] * 5,
        out_specs=(hbm, hbm),
        scratch_shapes=[vm((LEV, 8, 512), F32), dma((1 + 2 * OUT,))],
        compiler_params=pltpu.CompilerParams(vmem_limit_bytes=16 * 1024 * 1024),
        name="finish",
    )(*(pltpu.with_memory_space_constraint(a, pltpu.VMEM) for a in outs))


def solution(mesh):
    both = ("grp", "tile")
    in_specs = (
        P(None, both, None), P(None, both, None), P(both, None), P("tile", None),
        P(None, both, None), P(None, both, None), P(both, None, None, None),
        P(both, None), P(both, None), P(both, None),
    )
    out_specs = (P(None, both, None), P(None, both, None))
    return jax.shard_map(local, mesh=mesh, in_specs=in_specs, out_specs=out_specs, check_vma=False)
```

```python
import functools

import jax
import jax.numpy as jnp
from jax import lax
from jax.experimental import pallas as pl
from jax.experimental.pallas import tpu as pltpu
from jax.sharding import PartitionSpec as P

MESH = pl.DeviceIdType.MESH
F32 = jnp.float32
BF16 = jnp.bfloat16
F = 4
K = 4
LEV = 64
HALF = LEV // 2
TILES = 32
SLOTS = 8
MSG = 40
SENT = 33
CB = 4
WCH = 4
HR = 3 * LEV + 8
GAIN = 0.25
OUT = 4


def iota(shape, dim):
    return lax.broadcasted_iota(jnp.int32, shape, dim)


def one_hot(mask):
    return jnp.where(mask, 1.0, 0.0).astype(BF16)


def split(x):
    hi = x.astype(BF16)
    return hi, (x - hi.astype(F32)).astype(BF16)


def kernel(
    state_h, vert_h, nu_h, mask_h, coup_h, surf_h, w_h, dt_h, db_h, dg_h,
    ru_fwd, inv, ww, ends, rec_h,
    w_v, s0, st, ve, nu, mask, coup, surf, dt, db, dg,
    xs, terms, slab, got, ps, xr, es, xe,
    se, re, xh, coef, coef_h, wet, mid, rg, uu, gg,
    lsem, wsem, ssem, rsem, hs, hr, xss, xrs, ess, ers,
):
    grp = lax.axis_index("grp")
    tile = lax.axis_index("tile")
    dev = grp * TILES + tile
    ocean = grp == 3
    n_dev = 4 * TILES

    def dev_id(flat):
        return (flat // TILES, flat % TILES)

    above_dev = dev_id((dev + n_dev - 1) % n_dev)
    below_dev = dev_id((dev + 1) % n_dev)
    t_prev, t_next = (tile + TILES - 1) % TILES, (tile + 1) % TILES

    barrier = pltpu.get_barrier_semaphore()

    def tell(device):
        pl.semaphore_signal(barrier, inc=1, device_id=device, device_id_type=MESH)

    @pl.loop(1, TILES)
    def _(d):
        tell((grp, (tile + d) % TILES))

    tell(above_dev)
    tell(below_dev)

    @pl.when(ocean)
    def _():
        for g in range(3):
            for t in (tile, t_prev, t_next):
                tell((g, t))

    @pl.when(jnp.logical_not(ocean))
    def _():
        for t in (tile, t_prev, t_next):
            tell((3, t))

    def load(src, dst, i):
        return pltpu.make_async_copy(src, dst, lsem.at[i])

    small = [
        load(dt_h, dt, 0), load(db_h, db, 1), load(dg_h, dg, 2),
        load(mask_h, mask, 3), load(coup_h, coup, 4), load(surf_h, surf, 5), load(nu_h, nu, 6),
        load(state_h.at[0], s0, 15),
    ]
    st_load = [load(state_h.at[:, :, c * 128:(c + 1) * 128], st.at[c], 7 + c) for c in range(CB)]
    ve_load = [
        load(vert_h.at[:, :, c * 128:(c + 1) * 128], ve.at[c], 11 + c) for c in range(CB)
    ]
    per = 32 // WCH
    w_load = [
        pltpu.make_async_copy(w_h.at[pl.ds(i * per, per)], w_v.at[pl.ds(i * per, per)], wsem.at[i])
        for i in range(WCH)
    ]
    for d in small + w_load + st_load + ve_load:
        d.start()

    for d in small:
        d.wait()

    lane = iota((1, 128), 1)
    k_of = lane % 4
    b_of = 2 * ((lane % 64) // 4) + lane // 64
    group_label = jnp.where(ocean, 32, 0)
    both = jnp.concatenate(
        [((dt[...] + TILES - tile) % TILES).astype(F32),
         (db[...] + dg[...] * group_label + 1).astype(F32)], axis=0
    ).astype(BF16)
    wide = jnp.dot(both, one_hot(iota((32, 128), 0) == b_of), preferred_element_type=F32)
    of_k = iota((K, 128), 0) == k_of
    d_row = jnp.sum(jnp.where(of_k, wide[:K], 0.0), axis=0, keepdims=True)
    label = jnp.sum(jnp.where(of_k, wide[K:], 0.0), axis=0, keepdims=True)
    drel = d_row.astype(jnp.int32)
    i0, i1 = iota((128, 128), 0), iota((128, 128), 1)
    d_col = jnp.sum(jnp.where(i0 == i1, d_row, 0.0), axis=1, keepdims=True)
    pos = jnp.sum(jnp.where((d_col == d_row) & (i0 < i1), 1.0, 0.0), axis=0, keepdims=True)
    slot = drel * SLOTS + pos.astype(jnp.int32)
    tag_a = jnp.where(iota((TILES, 128), 0) == drel, label, 0.0).astype(BF16)
    tag_b = one_hot(i0 == slot % 128)
    tags = lax.dot_general(tag_a, tag_b, (((1,), (1,)), ((), ())), preferred_element_type=F32)
    for j in range(TILES // 8):
        slab[pl.ds(j * 8 * MSG + 32, 8, stride=MSG), :] = tags[j * 8:(j + 1) * 8]

    for c in range(CB):
        cs = slice(c * 128, (c + 1) * 128)
        wet_c = jnp.where(ocean, mask[:, cs].astype(F32), 1.0)
        wet[c] = wet_c
        for f in range(F):
            send = coup[f, :, cs] * (s0[:, cs] - surf[f, :, cs]) * wet_c
            xs[pl.ds(c * 4 + f, 8, stride=16), :] = send

    row8 = iota((8, 128), 0)

    def two_blocks(q):
        x8 = xs[pl.ds(q * 8, 8), :]
        x = jnp.concatenate(
            [jnp.where(row8 < 4, x8, 0.0), jnp.where(row8 < 4, 0.0, x8)], axis=1
        ).astype(BF16)
        for kp in range(2):
            cols = [w_v[pl.ds(2 * q, 2), 2 * kp + j].reshape(256, 128) for j in range(2)]
            t = jnp.dot(x, jnp.concatenate(cols, axis=1), preferred_element_type=F32)
            for j in range(2):
                terms[pl.ds(q * 4 + 2 * kp + j, 8, stride=64), :] = t[:, j * 128:(j + 1) * 128]

    for i in range(WCH):
        w_load[i].wait()
        for q in range(i * 16 // WCH, (i + 1) * 16 // WCH):
            two_blocks(q)

    his, los = [], []
    for f in range(F):
        t = jnp.concatenate([terms[bl * 256 + f * 64:bl * 256 + f * 64 + 64, :] for bl in range(2)], 0)
        hi, lo = split(t)
        his.append(hi)
        los.append(lo)
    hi = jnp.concatenate(his, axis=1)
    lo = jnp.concatenate(los, axis=1)

    def a2a(d):
        return pltpu.make_async_remote_copy(
            src_ref=slab.at[pl.ds(d * MSG, SENT)], dst_ref=got.at[pl.ds(d * MSG, SENT)],
            send_sem=ssem.at[d], recv_sem=rsem.at[d],
            device_id=(grp, (tile + d) % TILES), device_id_type=MESH,
        )

    parts = 4
    rows = TILES * SLOTS // parts
    for p in range(parts):
        ch = one_hot(iota((rows, 128), 0) + p * rows == slot)
        packed = jnp.dot(ch, hi, preferred_element_type=F32) + jnp.dot(
            ch, lo, preferred_element_type=F32
        )
        for j in range(TILES // parts):
            d = p * (TILES // parts) + j
            for f in range(F):
                slab[d * MSG + f * 8:d * MSG + f * 8 + 8, :] = packed[
                    j * 8:(j + 1) * 8, f * 128:(f + 1) * 128
                ]

    for d in st_load + ve_load:
        d.wait()
    for c in range(CB):
        rows = st.at[c].reshape(LEV * 8, 128)
        rows_v = ve.at[c].reshape((LEV - 1) * 8, 128)
        for side in range(2):
            near, far = 7 * side, 1 + 5 * side
            se[side, c, 0:LEV, :] = rows[pl.ds(near, LEV, stride=8), :]
            se[side, c, LEV:2 * LEV, :] = rows[pl.ds(far, LEV, stride=8), :]
            se[side, c, 2 * LEV:3 * LEV - 1, :] = rows_v[pl.ds(near, LEV - 1, stride=8), :]
            se[side, c, 3 * LEV:3 * LEV + 1, :] = wet[c, near:near + 1, :]
            se[side, c, 3 * LEV + 1:3 * LEV + 2, :] = wet[c, far:far + 1, :]
            se[side, c, 3 * LEV + 2:3 * LEV + 3, :] = nu[near:near + 1, c * 128:(c + 1) * 128]

    def halo(side):
        return pltpu.make_async_remote_copy(
            src_ref=se.at[side], dst_ref=re.at[side], send_sem=hs.at[side],
            recv_sem=hr.at[side], device_id=above_dev if side == 0 else below_dev,
            device_id_type=MESH,
        )

    @pl.when(ocean)
    def _():
        pl.semaphore_wait(barrier, 31 + 2 + 9)

    @pl.when(jnp.logical_not(ocean))
    def _():
        pl.semaphore_wait(barrier, 31 + 2 + 3)

    edge = [halo(side) for side in range(2)]
    to_above, to_below = (dev != 0) & (dev != 96), (dev != 127) & (dev != 95)
    from_above, from_below = (dev != 0) & (dev != 96), (dev != 127) & (dev != 95)

    @pl.when(to_above & (tile == 0))
    def _():
        edge[0].start()

    @pl.when(to_below & (tile == TILES - 1))
    def _():
        edge[1].start()

    @pl.loop(1, TILES)
    def _(d):
        a2a((d * 13) % TILES).start()

    @pl.when(tile != 0)
    def _():
        edge[0].start()

    @pl.when(tile != TILES - 1)
    def _():
        edge[1].start()

    inv[0, 0] = jnp.ones((8, 128), F32)
    inv[0, 1] = jnp.zeros((8, 128), F32)
    one, zero = inv[0, 0], inv[0, 1]
    wets = [wet[c] for c in range(CB)]

    def factor(i, carry):
        e_t, e_b, _, r_g = carry
        n_t, n_b, n_g = [], [], []
        for c in range(CB):
            a_t = ve[c, i] * wets[c]
            a_b = ve[c, LEV - 2 - i] * wets[c]
            i_t = 1.0 / (e_t[c] + a_t)
            i_b = 1.0 / (e_b[c] + a_b)
            w_t, w_b = a_t * i_t, a_b * i_b
            inv[c, i] = i_t
            inv[c, LEV - 1 - i] = i_b
            ww[c, i] = w_t
            ww[c, LEV - 1 - i] = w_b
            rg[c, i] = r_g[c]
            n_t.append(1.0 + w_t * e_t[c])
            n_b.append(1.0 + w_b * e_b[c])
            n_g.append(w_t * r_g[c])
        return n_t, n_b, e_b, n_g

    ones = [one] * CB
    zeros = [zero] * CB
    e_t, _, e_b, r_g = lax.fori_loop(0, HALF, factor, (ones, ones, ones, ones), unroll=4)
    mids = [1.0 / (e_t[c] + e_b[c] - 1.0) for c in range(CB)]
    for c in range(CB):
        mid[c] = mids[c]

    y_t, y_b = [], []
    for c in range(CB):
        y_t.append(r_g[c] * mids[c])
        y_b.append(inv[c, HALF - 1] * rg[c, HALF - 1] + ww[c, HALF - 1] * y_t[c])

    def back_g(i, carry):
        y_t, y_b = carry
        l_t, l_b = HALF - 1 - i, HALF + i
        n_t, n_b = [], []
        for c in range(CB):
            y0 = inv[c, l_t] * rg[c, l_t] + ww[c, l_t] * y_t[c]
            y1 = ww[c, l_b] * y_b[c]
            gg[c, l_t] = y0
            gg[c, l_b] = y1
            n_t.append(y0)
            n_b.append(y1)
        return n_t, n_b

    lax.fori_loop(0, HALF, back_g, (y_t, y_b), unroll=4)

    got[0:MSG, :] = slab[0:MSG, :]

    @pl.loop(1, TILES)
    def _(d):
        a2a(d).wait_recv()

    halves = []
    for h in range(2):
        t = got[pl.ds(h * 16 * MSG + 32, 8, stride=MSG), :] + got[
            pl.ds((h * 16 + 8) * MSG + 32, 8, stride=MSG), :
        ]
        halves.append(jnp.sum(t, axis=0, keepdims=True))
    tag_row = jnp.concatenate(halves, axis=1)
    m = iota((96, 256), 0)
    want = (m // 32) * 32 + (m % 8) * 4 + (m % 32) // 8 + 1
    ch2 = one_hot(want.astype(F32) == tag_row)
    for f in range(F):
        items = jnp.concatenate(
            [got[d * MSG + f * 8:d * MSG + f * 8 + 8, :] for d in range(TILES)], axis=0
        )
        hi, lo = split(items)
        part = jnp.dot(ch2, hi, preferred_element_type=F32) + jnp.dot(
            ch2, lo, preferred_element_type=F32
        )
        for g in range(3):
            for c in range(CB):
                ps[g, c, f] = part[g * 32 + c * 8:g * 32 + c * 8 + 8]
    for g in range(3):
        for c in range(CB):
            tot = ps[g, c, 0] + ps[g, c, 1] + ps[g, c, 2] + ps[g, c, 3]
            es[g, 0, c:c + 1, :] = tot[0:1]
            es[g, 1, c:c + 1, :] = tot[7:8]

    def across(g, src, to, j):
        return pltpu.make_async_remote_copy(
            src_ref=src, dst_ref=xr.at[j], send_sem=xss.at[g], recv_sem=xrs.at[j],
            device_id=to, device_id_type=MESH,
        )

    def across_edge(g, side, to, j):
        return pltpu.make_async_remote_copy(
            src_ref=es.at[g, side], dst_ref=xe.at[j, side], send_sem=ess.at[g, side],
            recv_sem=ers.at[j, side], device_id=to, device_id_type=MESH,
        )

    def ocean_sends():
        copies = []
        for g in (1, 0, 2):
            copies.append(across_edge(g, 0, dev_id((g * TILES + tile + 95) % 96), 0))
            copies.append(across_edge(g, 1, dev_id((g * TILES + tile + 1) % 96), 0))
            copies.append(across(g, ps.at[g], (g, tile), 0))
        return copies

    def air_sends():
        return [
            across_edge(0, 0, (3, t_prev), grp),
            across_edge(0, 1, (3, t_next), grp),
            across(0, ps.at[0], (3, tile), grp),
        ]

    @pl.when(ocean)
    def _():
        for d in ocean_sends():
            d.start()

    @pl.when(jnp.logical_not(ocean))
    def _():
        for d in air_sends():
            d.start()
        for j in range(1, 3):
            xr[j] = jnp.zeros(xr.shape[1:], F32)
            xe[j] = jnp.zeros(xe.shape[1:], F32)

    @pl.when(from_below)
    def _():
        edge[0].wait_recv()

    @pl.when(from_above)
    def _():
        edge[1].wait_recv()

    lane8 = iota((8, 128), 1)
    keep_above = jnp.where((dev != 0) & (dev != 96), 1.0, 0.0)
    keep_below = jnp.where((dev != 127) & (dev != 95), 1.0, 0.0)

    def neighbours(x, up, dn):
        ls = [pltpu.roll(x[c], 1, 1) for c in range(CB)]
        rs = [pltpu.roll(x[c], 127, 1) for c in range(CB)]
        out = []
        for c in range(CB):
            left = ls[c] if c == 0 else jnp.where(lane8 == 0, ls[c - 1], ls[c])
            right = rs[c] if c == CB - 1 else jnp.where(lane8 == 127, rs[c + 1], rs[c])
            above = jnp.where(row8 == 0, up[c], pltpu.roll(x[c], 1, 0))
            below = jnp.where(row8 == 7, dn[c], pltpu.roll(x[c], 7, 0))
            out.append((left, right, above, below))
        return out

    wet_up = [re[1, c, 3 * LEV:3 * LEV + 1, :] for c in range(CB)]
    wet_dn = [re[0, c, 3 * LEV:3 * LEV + 1, :] for c in range(CB)]
    around = neighbours(
        wets, [w * keep_above for w in wet_up], [w * keep_below for w in wet_dn]
    )
    for c in range(CB):
        left, right, above, below = around[c]
        if c == 0:
            left = jnp.where(lane8 == 0, 0.0, left)
        if c == CB - 1:
            right = jnp.where(lane8 == 127, 0.0, right)
        scale = nu[:, c * 128:(c + 1) * 128] * wets[c]
        cs = [scale * v for v in (left, right, above, below)]
        for j in range(4):
            coef[j, c] = cs[j]
        coef[4, c] = 1.0 - (cs[0] + cs[1] + cs[2] + cs[3])

    def spread(x, up, dn):
        out = []
        for c, near in enumerate(neighbours(x, up, dn)):
            total = coef[4, c] * x[c]
            for j in range(4):
                total = total + coef[j, c] * near[j]
            out.append(total)
        return out

    re_rows = re.reshape(2 * CB * HR, 128)
    se_rows = se.reshape(2 * CB * HR, 128)

    def theirs(row):
        return re_rows[pl.ds(row, 8, stride=HR), :]

    def mine(row):
        return pltpu.roll(se_rows[pl.ds(row, 8, stride=HR), :], 4, 0)

    def sideways(x):
        left, right = pltpu.roll(x, 1, 1), pltpu.roll(x, 127, 1)
        left = jnp.where(lane8 == 0, pltpu.roll(left, 1, 0), left)
        right = jnp.where(lane8 == 127, pltpu.roll(right, 7, 0), right)
        return left, right

    wet_h = theirs(3 * LEV)
    left, right = sideways(wet_h)
    left = jnp.where((lane8 == 0) & (row8 % 4 == 0), 0.0, left)
    right = jnp.where((lane8 == 127) & (row8 % 4 == 3), 0.0, right)
    scale = theirs(3 * LEV + 2) * wet_h
    ch = [scale * left, scale * right, scale * theirs(3 * LEV + 1), scale * mine(3 * LEV)]
    ch.append(1.0 - (ch[0] + ch[1] + ch[2] + ch[3]))
    for j in range(5):
        coef_h[j] = ch[j]

    def spread_h(l):
        x = theirs(l)
        left, right = sideways(x)
        return (
            coef_h[4] * x + coef_h[0] * left + coef_h[1] * right
            + coef_h[2] * theirs(LEV + l) + coef_h[3] * mine(l)
        )

    def halo_rows(side, l):
        return [re[side, c, pl.ds(l, 1), :] for c in range(CB)]

    def first(i, carry):
        r_t, r_b, e_t, e_b, _, r_g = carry
        l_t, l_b = i, LEV - 1 - i
        a_t = theirs(2 * LEV + i) * wet_h
        a_b = theirs(3 * LEV - 2 - i) * wet_h
        i_t = 1.0 / (e_t + a_t)
        i_b = 1.0 / (e_b + a_b)
        w_t, w_b = a_t * i_t, a_b * i_b
        inv[CB, l_t] = i_t
        inv[CB, l_b] = i_b
        ww[CB, l_t] = w_t
        ww[CB, l_b] = w_b
        rg[CB, l_t] = r_g
        h_t = spread([st[c, l_t] for c in range(CB)], halo_rows(1, l_t), halo_rows(0, l_t))
        h_b = spread([st[c, l_b] for c in range(CB)], halo_rows(1, l_b), halo_rows(0, l_b))
        h_t.append(spread_h(l_t))
        h_b.append(spread_h(l_b))
        n_t, n_b = [], []
        for c in range(CB + 1):
            r = h_t[c] + r_t[c]
            s = h_b[c] + r_b[c]
            ru_fwd[c, l_t] = r
            ru_fwd[c, l_b] = s
            n_t.append((ww[c, l_t] if c < CB else w_t) * r)
            n_b.append((ww[c, l_b] if c < CB else w_b) * s)
        return n_t, n_b, 1.0 + w_t * e_t, 1.0 + w_b * e_b, e_b, w_t * r_g

    r_t, _, e_t, _, e_b, r_g = lax.fori_loop(
        0, HALF, first, (zeros + [zero], zeros + [zero], one, one, one, one), unroll=4
    )
    mid_h = 1.0 / (e_t + e_b - 1.0)
    x_b, x_t = [], []
    for c in range(CB + 1):
        x_t.append((ru_fwd[c, HALF] + r_t[c]) * (mids[c] if c < CB else mid_h))
        x_b.append(inv[c, HALF - 1] * ru_fwd[c, HALF - 1] + ww[c, HALF - 1] * x_t[c])
    y_t = r_g * mid_h
    y_b = inv[CB, HALF - 1] * rg[CB, HALF - 1] + ww[CB, HALF - 1] * y_t

    def back(i, carry):
        x_t, x_b, y_t, y_b = carry
        l_t, l_b = HALF - 1 - i, HALF + i
        n_t, n_b = [], []
        for c in range(CB + 1):
            w_t, w_b, i_t, i_b = ww[c, l_t], ww[c, l_b], inv[c, l_t], inv[c, l_b]
            x0 = i_t * ru_fwd[c, l_t] + w_t * x_t[c]
            x1 = i_b * ru_fwd[c, l_b] + w_b * x_b[c]
            uu[c, l_t] = x0
            uu[c, l_b] = x1
            n_t.append(x0)
            n_b.append(x1)
        y0 = i_t * rg[CB, l_t] + w_t * y_t
        y1 = w_b * y_b
        gg[CB, l_t] = y0
        gg[CB, l_b] = y1
        return n_t, n_b, y0, y1

    lax.fori_loop(0, HALF, back, (x_t, x_b, y_t, y_b), unroll=4)

    @pl.when(ocean)
    def _():
        for j in range(3):
            across(j, ps.at[0], (0, tile), j).wait_recv()
            for side in range(2):
                across_edge(j, side, (0, tile), j).wait_recv()

    @pl.when(jnp.logical_not(ocean))
    def _():
        across(0, ps.at[0], (3, tile), 0).wait_recv()
        for side in range(2):
            across_edge(0, side, (3, tile), 0).wait_recv()

    forc = []
    e_up = (xe[0, 1] + xe[1, 1] + xe[2, 1]) * GAIN
    e_dn = (xe[0, 0] + xe[1, 0] + xe[2, 0]) * GAIN
    for c in range(CB):
        tot = None
        for f in range(F):
            r = xr[0, c, f] + xr[1, c, f] + xr[2, c, f]
            rec_h[f, :, c * 128:(c + 1) * 128] = r
            tot = r if tot is None else tot + r
        forc.append(GAIN * wets[c] * tot)
    f_h = jnp.where(row8 < 4, e_dn, pltpu.roll(e_up, 4, 0)) * wet_h
    for l in range(LEV):
        xh[l] = uu[CB, l] + gg[CB, l] * f_h


    def level(l):
        x = [uu[c, l] + gg[c, l] * forc[c] for c in range(CB)]
        up = [xh[l, 4 + c:5 + c, :] for c in range(CB)]
        dn = [xh[l, c:c + 1, :] for c in range(CB)]
        return spread(x, up, dn)

    def second(i, carry):
        r_t, r_b = carry
        l_t, l_b = i, LEV - 1 - i
        h_t, h_b = level(l_t), level(l_b)
        n_t, n_b = [], []
        for c in range(CB):
            r = h_t[c] + r_t[c]
            s = h_b[c] + r_b[c]
            ru_fwd[c, l_t] = r
            ru_fwd[c, l_b] = s
            n_t.append(ww[c, l_t] * r)
            n_b.append(ww[c, l_b] * s)
        return n_t, n_b

    r_t, _ = lax.fori_loop(0, HALF, second, (forc, zeros), unroll=8)
    for c in range(CB):
        x32 = (ru_fwd[c, HALF] + r_t[c]) * mid[c]
        ends[0, c] = x32
        ends[1, c] = inv[c, HALF - 1] * ru_fwd[c, HALF - 1] + ww[c, HALF - 1] * x32

    @pl.when(to_above)
    def _():
        edge[0].wait_send()

    @pl.when(to_below)
    def _():
        edge[1].wait_send()


    @pl.loop(1, TILES)
    def _(d):
        a2a(d).wait_send()

    @pl.when(ocean)
    def _():
        for d in ocean_sends():
            d.wait_send()

    @pl.when(jnp.logical_not(ocean))
    def _():
        for d in air_sends():
            d.wait_send()


def finish(fwd, inv, ww, ends, received_v, state_h, received_h, out, sem):
    copies = [pltpu.make_async_copy(received_v, received_h, sem.at[0])]
    copies[0].start()
    step = HALF // OUT

    def back(i, carry):
        x_t, x_b = carry
        l_t, l_b = HALF - 1 - i, HALF + i
        n_t, n_b = [], []
        for c in range(CB):
            cs = slice(c * 128, (c + 1) * 128)
            x0 = inv[c, l_t] * fwd[c, l_t] + ww[c, l_t] * x_t[c]
            x1 = inv[c, l_b] * fwd[c, l_b] + ww[c, l_b] * x_b[c]
            out[l_t, :, cs] = x0
            out[l_b, :, cs] = x1
            n_t.append(x0)
            n_b.append(x1)
        return n_t, n_b

    carry = ([ends[0, c] for c in range(CB)], [ends[1, c] for c in range(CB)])
    for j in range(OUT):
        carry = lax.fori_loop(j * step, (j + 1) * step, back, carry, unroll=step)
        for half, first in enumerate((HALF - (j + 1) * step, HALF + j * step)):
            rows = pl.ds(first, step)
            d = pltpu.make_async_copy(out.at[rows], state_h.at[rows], sem.at[1 + 2 * j + half])
            d.start()
            copies.append(d)
    for d in copies:
        d.wait()


def local(*args):
    vm = pltpu.VMEM
    dma = pltpu.SemaphoreType.DMA
    col = (CB, LEV, 8, 128)
    five = (CB + 1, LEV, 8, 128)
    scratch = [
        vm((32, K, 128, 128), BF16), vm((8, 512), F32), vm(col, F32), vm((CB, LEV - 1, 8, 128), F32),
        vm((8, 512), F32), vm((8, 512), jnp.int32), vm((F, 8, 512), F32), vm((F, 8, 512), F32),
        vm((K, 32), jnp.int32), vm((K, 32), jnp.int32), vm((K, 32), jnp.int32),
        vm((128, 128), F32), vm((512, 128), F32),
        vm((TILES * MSG, 128), F32), vm((TILES * MSG, 128), F32),
        vm((3, CB, F, 8, 128), F32), vm((3, CB, F, 8, 128), F32),
        vm((3, 2, 8, 128), F32), vm((3, 2, 8, 128), F32),
        vm((2, CB, HR, 128), F32), vm((2, CB, HR, 128), F32), vm((LEV, 8, 128), F32),
        vm((5, CB, 8, 128), F32), vm((5, 8, 128), F32), vm((CB, 8, 128), F32),
        vm((CB, 8, 128), F32),
        vm((CB + 1, HALF, 8, 128), F32), vm(five, F32), vm(five, F32),
        dma((16,)), dma((WCH,)), dma((TILES,)), dma((TILES,)), dma((2,)), dma((2,)),
        dma((3,)), dma((3,)), dma((3, 2)), dma((3, 2)),
    ]
    hbm = pl.BlockSpec(memory_space=pltpu.HBM)
    out = pl.BlockSpec(memory_space=pltpu.VMEM)
    outs = pl.pallas_call(
        kernel,
        out_shape=(
            vm(five, F32), vm(five, F32), vm(five, F32), vm((2, CB, 8, 128), F32),
            vm((F, 8, 512), F32),
        ),
        in_specs=[hbm] * 10,
        out_specs=(out,) * 5,
        scratch_shapes=scratch,
        compiler_params=pltpu.CompilerParams(
            collective_id=0, has_side_effects=True, vmem_limit_bytes=50 * 1024 * 1024
        ),
        name="window",
    )(*(pltpu.with_memory_space_constraint(a, pltpu.HBM) for a in (*args[:7], *(a.T for a in args[7:]))))
    return pl.pallas_call(
        finish,
        out_shape=(
            jax.ShapeDtypeStruct((LEV, 8, 512), F32), jax.ShapeDtypeStruct((F, 8, 512), F32),
        ),
        in_specs=[pl.BlockSpec(memory_space=pltpu.VMEM)] * 5,
        out_specs=(hbm, hbm),
        scratch_shapes=[vm((LEV, 8, 512), F32), dma((1 + 2 * OUT,))],
        compiler_params=pltpu.CompilerParams(vmem_limit_bytes=16 * 1024 * 1024),
        name="finish",
    )(*(pltpu.with_memory_space_constraint(a, pltpu.VMEM) for a in outs))


def solution(mesh):
    both = ("grp", "tile")
    in_specs = (
        P(None, both, None), P(None, both, None), P(both, None), P("tile", None),
        P(None, both, None), P(None, both, None), P(both, None, None, None),
        P(both, None), P(both, None), P(both, None),
    )
    out_specs = (P(None, both, None), P(None, both, None))
    return jax.shard_map(local, mesh=mesh, in_specs=in_specs, out_specs=out_specs, check_vma=False)
```
